32 devices in a mesh: groups: 2 (over y), store: 4 (over x, core), tensor: 4 (over z).
Axes of the slice: x: 2, y: 2, z: 4, core: 2. Of those that a mesh axis runs over, the one named last changes fastest.
Arguments:
- cached_rows: bfloat16 [8, 2048, 8192], P(('groups', 'store'), None, 'tensor'), parts along dimension 0, may hold values from -400 to 400
- counts: int32 [8], P(('groups', 'store')), parts along dimension 0, may hold values from 0 to 16, as said below
- dest_table: int32 [8, 16], P(('groups', 'store')), parts along dimension 0, may hold values from -1 to 31, as said below
- positions: int32 [8192], P(('groups', 'store')), parts along dimension 0, may hold values from 0 to 32767
- norm_gain: float32 [8192], replicated, may hold values from 0.1 to 1.9
- key_weight: bfloat16 [8192, 4096], P(None, 'tensor'), may hold values from -0.0625 to 0.0625
- value_weight: bfloat16 [8192, 4096], P(None, 'tensor'), may hold values from -0.0625 to 0.0625
- key_bias: float32 [4096], P('tensor'), may hold values from -4 to 4
- value_bias: float32 [4096], P('tensor'), may hold values from -4 to 4
Outputs:
- key_out: bfloat16 [8192, 4096], P(('groups', 'store'), 'tensor'), parts along dimension 0
- value_out: bfloat16 [8192, 4096], P(('groups', 'store'), 'tensor'), parts along dimension 0
The draws below stay inside these ranges and needn't reach their ends.
There are 2 independent parts, one for each index of `groups`. The reference program is written for one: setup_inputs(seed, part) draws one part's arguments, and reference() takes and returns one part's arrays. A program takes and returns all parts, laid end to end along the dimension named above; an argument that names none is the same for every part. Nothing has to cross between parts.
Inputs may be any that keep to these rules, and one draw needn't show every extreme that they name: `counts`: one store device holds 16 blocks; they sum to 32 over the store devices. `dest_table`: slots below a device's count name each of the 32 blocks exactly once over all store devices; slots beyond it hold -1. A device holds at most 4 blocks that belong to one index of store (blocks b with b // 8 equal), and one device holds exactly 4 for every index; a device's valid slots run in order of that index.
All inputs are finite; a program needn't handle non-finite values.
Results may differ from the reference program's by a relative error of at most 0.0041.
Values may be sent and summed in bfloat16 or wider, within the bound.
No kernel may reach another device: no remote copies, remote signals or barrier semaphores. Data moves between devices by JAX's collectives and lax.ppermute only.
A program may use at most 192 MiB of HBM per device.

```python
import math
import jax
import jax.numpy as jnp
from jax import lax

D = 8192
HEADS = 32
HD = 128
BLOCK = 128
BPR = 8
MOST = 4
CAP = 16
NBLK = 32
TOKENS = 4096
N_STORE = 4


def block_layout(key):
    heavy_source = jax.random.randint(jax.random.fold_in(key, 1), (), 0, N_STORE).astype(jnp.int32)
    row_keys = jax.random.split(jax.random.fold_in(key, 2), N_STORE)
    spare_slots = (N_STORE - 1) * MOST

    def one_row(row_key):
        first_key, second_key = jax.random.split(row_key)
        slot_order = jax.random.permutation(first_key, spare_slots)[:BPR - MOST] // MOST
        slot_order = slot_order.astype(jnp.int32)
        others = slot_order + (slot_order >= heavy_source).astype(jnp.int32)
        sources = jnp.concatenate([jnp.full((MOST,), 1, jnp.int32) * heavy_source, others])
        blocks = jax.random.permutation(second_key, BPR).astype(jnp.int32)
        return (sources, blocks)
    sources, blocks = jax.vmap(one_row)(row_keys)
    blocks = blocks + (jnp.arange(N_STORE, dtype=jnp.int32) * BPR)[:, None]
    sources = sources.reshape(-1)
    blocks = blocks.reshape(-1)
    onehot = (sources[:, None] == jnp.arange(N_STORE, dtype=jnp.int32)[None, :]).astype(jnp.int32)
    slot_rank = jnp.sum((jnp.cumsum(onehot, axis=0) - onehot) * onehot, axis=1)
    counts = jnp.sum(onehot, axis=0).astype(jnp.int32)
    dest_table = jnp.full((N_STORE, CAP), -1, jnp.int32).at[sources, slot_rank].set(blocks)
    return (counts, dest_table)


def draw_counts(key, part):
    counts, dest_table = block_layout(key)
    return counts


def draw_dest_table(key, part):
    counts, dest_table = block_layout(key)
    return dest_table


def draw_cached_rows(key, part):
    key = jax.random.fold_in(key, 11)
    base_key, row_key, col_key = jax.random.split(key, 3)
    shape = (N_STORE, CAP * BLOCK, D)
    values = jnp.clip(jax.random.normal(base_key, shape, jnp.float32), -4.0, 4.0)
    col_top = math.log(10.0)
    row_scale = jnp.exp(jax.random.uniform(row_key, (N_STORE, CAP * BLOCK, 1), jnp.float32, 0.0, math.log(10.0)))
    col_scale = jnp.exp(jax.random.uniform(col_key, (D,), jnp.float32, 0.0, col_top))
    values = values * row_scale * col_scale[None, None, :]
    return jnp.clip(values, -400.0, 400.0).astype(jnp.bfloat16)


def with_ends(drawn, rng, smallest, largest):
    dims = drawn.shape
    spot = [jax.random.randint(jax.random.fold_in(rng, axis), (), 0, dims[axis]) for axis in range(len(dims))]
    drawn = drawn.at[tuple(spot)].set(smallest)
    longest = dims.index(max(dims))
    spot[longest] = (spot[longest] + 1) % dims[longest]
    return drawn.at[tuple(spot)].set(largest)


def steps_of(rng, extent, shards, least, high):
    loudness = 1.0
    for position, parts in shards:
        steps = jax.random.uniform(jax.random.fold_in(jax.random.fold_in(rng, 6), position), (parts,), jnp.float32, least / len(shards), high / len(shards))
        loudness = loudness * jnp.repeat(jnp.exp(steps), extent[position] // parts).reshape((-1,) + (1,) * (len(extent) - 1 - position))
    return loudness


def centred(rng, dims, spread, bound, shards=(), kind=jnp.bfloat16):
    factor_of = steps_of(rng, dims, shards, -0.22, 0.18) if shards else 1.0
    values = jax.random.normal(rng, dims, jnp.float32) * spread * factor_of
    return jnp.minimum(jnp.maximum(values, -bound), bound).astype(kind)


def setup_inputs(seed: int = 0, part: int = 0) -> dict:
    key_of = jax.random.split(jax.random.key(seed), 10)
    own_keys = jax.random.split(jax.random.fold_in(key_of[9], part), 10)
    cached_rows = draw_cached_rows(jax.random.fold_in(jax.random.fold_in(key_of[9], part), 71), part)
    counts = draw_counts(jax.random.fold_in(jax.random.fold_in(key_of[9], part), 71), part)
    dest_table = draw_dest_table(jax.random.fold_in(jax.random.fold_in(key_of[9], part), 71), part)
    positions = with_ends(jax.random.randint(own_keys[3], (TOKENS,), 0, 32768), jax.random.fold_in(own_keys[3], 1), 0, 32767).astype(jnp.int32)
    norm_gain = jnp.clip(1.0 + 0.18 * jax.random.normal(key_of[4], (D,), jnp.float32), 0.1, 1.9)
    key_weight = centred(key_of[5], (D, HEADS * HD), D ** -0.5, 0.0625, ((1, 4),))
    value_weight = centred(key_of[6], (D, HEADS * HD), D ** -0.5, 0.0625, ((1, 4),))
    key_bias = centred(key_of[7], (HEADS * HD,), 1.0, 4.0, ((0, 4),), jnp.float32)
    value_bias = centred(key_of[8], (HEADS * HD,), 1.0, 4.0, ((0, 4),), jnp.float32)
    return {"cached_rows": cached_rows, "counts": counts, "dest_table": dest_table, "positions": positions, "norm_gain": norm_gain, "key_weight": key_weight, "value_weight": value_weight, "key_bias": key_bias, "value_bias": value_bias}


rope_base = 1000000.0

def rotate_keys(key_raw, positions):
    heads_here = key_raw.shape[1] // HD
    half_size = HD // 2
    per_head = key_raw.reshape(key_raw.shape[0], heads_here, HD)
    inverse = 1.0 / rope_base ** (jnp.arange(half_size, dtype=jnp.float32) * 2.0 / HD)
    angles = positions.astype(jnp.float32)[:, None] * inverse[None, :]
    cosine = jnp.cos(angles)[:, None, :]
    sine_part = jnp.sin(angles)[:, None, :]
    first_half = per_head[:, :, :half_size]
    second_half = per_head[:, :, half_size:]
    rotated = jnp.concatenate([first_half * cosine - second_half * sine_part, second_half * cosine + first_half * sine_part], axis=2)
    return rotated.reshape(key_raw.shape[0], heads_here * HD)

def reference(cached_rows, counts, dest_table, positions, norm_gain, key_weight, value_weight, key_bias, value_bias):
    slot_ids = jnp.arange(CAP, dtype=jnp.int32)
    is_valid = slot_ids[None, :] < counts[:, None]
    target_ids = jnp.where(is_valid, dest_table, NBLK).reshape(-1).astype(jnp.int32)
    blocks = cached_rows.reshape(N_STORE * CAP, BLOCK, D)
    placed = jnp.zeros((NBLK, BLOCK, D), cached_rows.dtype).at[target_ids].set(blocks, mode='drop')
    layer_input = placed.reshape(TOKENS, D).astype(jnp.float32)
    mean_square = lax.optimization_barrier(jnp.mean(layer_input * layer_input, axis=1))
    inv_scale = lax.rsqrt(mean_square + 1e-06)
    normed = (layer_input * inv_scale[:, None] * norm_gain[None, :]).astype(jnp.bfloat16)
    key_raw = jnp.dot(normed, key_weight, preferred_element_type=jnp.float32) + key_bias[None, :]
    value_out = (jnp.dot(normed, value_weight, preferred_element_type=jnp.float32) + value_bias[None, :]).astype(jnp.bfloat16)
    key_out = rotate_keys(key_raw, positions).astype(jnp.bfloat16)
    return (key_out, value_out)
```

```python
import collections
import functools

import jax
import jax.numpy as jnp
from jax import lax
from jax.experimental import pallas as pl
from jax.experimental.pallas import tpu as pltpu
from jax.sharding import PartitionSpec as P

HD = 128
BLOCK = 128
ROPE_BASE = 1000000.0
EPS = 1e-06
MIB = 1 << 20
VMEM_LIMIT = 63 * MIB
COST = 4 * 10**9
FAR = 10**11
HBM = pl.BlockSpec(memory_space=pltpu.HBM)
SMEM = pl.BlockSpec(memory_space=pltpu.SMEM)
VMEM = pl.BlockSpec(memory_space=pltpu.VMEM)
TOKEN = jax.ShapeDtypeStruct((8, 128), jnp.int32)

STEPS = ((0, 0, 64), (0, 64, 64), (1, 0, 128), (2, 0, 128), (3, 0, 128))
CHUNKS = ((0, 0, 64), (0, 64, 64), (1, 0, 128), (2, 0, 128), (3, 0, 128))


def rope_tables(positions):
    half = HD // 2
    inverse = 1.0 / ROPE_BASE ** (jnp.arange(half, dtype=jnp.float32) * 2.0 / HD)
    angles = positions.astype(jnp.float32)[:, None] * inverse[None, :]
    cosine, sine = jnp.cos(angles), jnp.sin(angles)
    return (
        jnp.concatenate([cosine, cosine], axis=1),
        jnp.concatenate([-sine, sine], axis=1),
    )


class Chain:
    def __init__(self):
        self.token = None

    def __call__(self, kernel, name, args, specs, outs, out_specs, scratch=(), grid=None, aliases=None, cost=COST):
        first = self.token is None
        prefetch = 0 if grid is None else 1
        taken, given = len(args), len(outs)

        def body(*refs):
            ins = refs[:taken]
            after = taken + (0 if first else 1)
            kernel(*ins, *refs[after : after + given], *refs[after + given + 1 :])

        tokens = () if first else (self.token,)
        in_specs = list(specs) + [HBM] * len(tokens)
        out_specs = list(out_specs) + [HBM]
        if grid is None:
            where = dict(in_specs=in_specs, out_specs=out_specs, scratch_shapes=list(scratch))
        else:
            where = dict(
                grid_spec=pltpu.PrefetchScalarGridSpec(
                    num_scalar_prefetch=prefetch,
                    grid=grid,
                    in_specs=in_specs,
                    out_specs=out_specs,
                    scratch_shapes=list(scratch),
                )
            )
        result = pl.pallas_call(
            body,
            out_shape=tuple(outs) + (TOKEN,),
            input_output_aliases=aliases or {},
            compiler_params=pltpu.CompilerParams(vmem_limit_bytes=VMEM_LIMIT),
            cost_estimate=pl.CostEstimate(flops=cost, bytes_accessed=1, transcendentals=0),
            name=name,
            **where,
        )(*args, *tokens)
        self.token = result[-1]
        return result[:-1]

    def pin(self, name, arrays, cost=COST):
        outs = [jax.ShapeDtypeStruct(a.shape, a.dtype) for a in arrays]
        n = len(arrays)
        return self(
            lambda *refs: None, name, arrays, [HBM] * n, outs, [HBM] * n, aliases={i: i for i in range(n)}, cost=cost
        )


def in_row(table, low, per_row):
    start, count = jnp.int32(0), jnp.int32(0)
    for s in range(table.shape[1]):
        block = table[0, s]
        start += ((block >= 0) & (block < low)).astype(jnp.int32)
        count += ((block >= low) & (block < low + per_row)).astype(jnp.int32)
    return start, count


def plan_kernel(stores, per_row, *refs):
    tables, plan = refs[:-1], refs[-1]
    low = lax.axis_index("store") * per_row
    spans = [in_row(t, low, per_row) for t in tables]
    n = jnp.int32(0)
    for i in range(per_row):
        for f in range(3):
            plan[i, f] = jnp.int32(0)
    for r in range(tables[0].shape[1] // stores):
        for m in range(stores):
            start, count = spans[m]
            valid = r < count

            @pl.when(valid)
            def _():
                plan[n, 0] = jnp.int32(r * stores + m)
                plan[n, 1] = start + r
                plan[n, 2] = tables[m][0, start + r] - low

            n += valid.astype(jnp.int32)


def send_kernel(steps, per_row, table, cached, *refs):
    outs, sems = refs[:-1], refs[-1]
    own_row = lax.axis_index("store")
    last = table.shape[1] - 1
    starts = {m: in_row(table, (own_row ^ m) * per_row, per_row)[0] for m in {m for s in steps for _, m, _ in s}}
    copies = []
    for out, parts in zip(outs, steps):
        for at, m, (k, low, rows) in parts:
            src = pl.multiple_of(jnp.minimum(starts[m] + k, last) * BLOCK + low, 16)
            copies.append(
                pltpu.make_async_copy(cached.at[pl.ds(src, rows)], out.at[pl.ds(at, rows)], sems.at[len(copies)])
            )
            copies[-1].start()
    for c in copies:
        c.wait()


def cut_kernel(key_weight, value_weight, out, sems):
    z, y, own_row = lax.axis_index("tensor"), lax.axis_index("groups"), lax.axis_index("store")
    share = out.shape[0] // 2
    slab = jnp.where(z == 0, 2 + y, 1 - y)
    at = pl.multiple_of((slab * 4 + own_row) * share, 128)
    copies = [
        pltpu.make_async_copy(weight.at[pl.ds(at, share)], out.at[pl.ds(g * share, share)], sems.at[g])
        for g, weight in enumerate((key_weight, value_weight))
    ]
    for c in copies:
        c.start()
    for c in copies:
        c.wait()


def split_kernel(both, keys, values, sems):
    share = keys.shape[0]
    copies = [
        pltpu.make_async_copy(both.at[pl.ds(g * share, share)], out, sems.at[g])
        for g, out in enumerate((keys, values))
    ]
    for c in copies:
        c.start()
    for c in copies:
        c.wait()


def join_kernel(info, *refs):
    all_out, sems = refs[6], refs[7]
    copies = []
    for g, out in enumerate(refs[4:6]):
        share = out.shape[0] // 2
        place = info[5 + g]
        for t, src in enumerate(refs[2 * g : 2 * g + 2]):
            at = pl.multiple_of((place if t == 0 else 1 - place) * share, 128)
            copies.append(pltpu.make_async_copy(src, out.at[pl.ds(at, share)], sems.at[0, g, t]))
            there = all_out.at[pl.ds(at + 2 * g * share, share)]
            copies.append(pltpu.make_async_copy(src, there, sems.at[1, g, t]))
    for c in copies:
        c.start()
    for c in copies:
        c.wait()


def prep_kernel(low, rows, first, stores, pieces, plan, cached, *refs):
    arrived = refs[: len(pieces)]
    gain, y_out, ssq_out, held, sems = refs[len(pieces) :]
    width = held.shape[2]
    for j in range(2):
        code = plan[first + j, 0]

        @pl.when(lax.rem(code, stores) == 0)
        def _():
            start = pl.multiple_of(plan[first + j, 1] * BLOCK + low, 16)
            pltpu.make_async_copy(cached.at[pl.ds(start, rows)], held.at[j], sems.at[j]).start()

        for (r, m, p_low, p_rows, at), ref in zip(pieces, arrived):
            a, b = max(low, p_low), min(low + rows, p_low + p_rows)

            @pl.when(code == r * stores + m)
            def _():
                pltpu.make_async_copy(
                    ref.at[pl.ds(at + a - p_low, b - a)], held.at[j, pl.ds(a - low, b - a)], sems.at[j]
                ).start()

    for j in range(2):
        pltpu.make_async_copy(cached.at[pl.ds(0, rows)], held.at[j], sems.at[j]).wait()
        sums = jnp.zeros((rows, 128), jnp.float32)
        for c in range(0, width, 128):
            x = held[j, :, c : c + 128].astype(jnp.float32)
            y_out[j * rows : (j + 1) * rows, c : c + 128] = (x * gain[:, c : c + 128]).astype(jnp.bfloat16)
            sums += x * x
        ssq_out[j : j + 1, :rows] = jnp.sum(sums.T, axis=0, keepdims=True)


def sums_kernel(step, *refs):
    out = refs[-1]
    if step == 0:
        out[...] = jnp.zeros_like(out)
        for i, ref in enumerate(refs[:-1]):
            out[2 * i : 2 * i + 2, :] = ref[...]
    else:
        out[...] = refs[0][...] + refs[1][...]


def relay_kernel(own, ex, out, sems):
    rows = own.shape[0]
    copies = [
        pltpu.make_async_copy(src, out.at[pl.ds(i * rows, rows)], sems.at[i]) for i, src in enumerate((own, ex))
    ]
    for c in copies:
        c.start()
    for c in copies:
        c.wait()


def near_kernel(sizes, first, handed, info, *refs):
    n = len(sizes)
    wk, wv, acc, acts, sems = refs[-5:]
    arrays = refs[:-5]
    per = len(arrays) // n
    slabs = acts.shape[0]
    i = pl.program_id(0)
    slab, half = first + i // 2, lax.rem(i, 2)
    inner = info[4] == 1
    full = (i >= 0) if handed else inner
    starts = [sum(sizes[:c]) for c in range(n)]

    def copies(s, which, skip=0):
        return [
            pltpu.make_async_copy(
                arrays[per * c + which].at[pl.ds(skip * sizes[c], sizes[c])],
                acts.at[s - first, pl.ds(starts[c], sizes[c])],
                sems.at[s - first, c],
            )
            for c in range(n)
        ]

    @pl.when(i == 0)
    def _():
        for s in range(first, first + slabs):
            if s < 2:
                for c in copies(s, s):
                    c.start()
            else:

                @pl.when(inner)
                def _():
                    for c in copies(s, 2 - first, s - 2):
                        c.start()

                if handed:

                    @pl.when(jnp.logical_not(inner))
                    def _():
                        for c in copies(s, 3 - first, s - 2):
                            c.start()

    for s in range(first, first + slabs):

        @pl.when((half == 0) & (slab == s) & ((s < 2) | full))
        def _():
            for c in copies(s, 0):
                c.wait()

    part, cols = wk.shape

    @pl.when(i == 0)
    def _():
        if first >= 2 and not handed:
            acc[...] = jnp.zeros_like(acc)

        @pl.when((first < 2) | full)
        def _():
            a = acts[0, :, :part]
            acc[:, :cols] = jnp.dot(a, wk[...], preferred_element_type=jnp.float32)
            acc[:, cols:] = jnp.dot(a, wv[...], preferred_element_type=jnp.float32)

    @pl.when((i > 0) & ((slab < 2) | full))
    def _():
        a = acts[slab - first, :, pl.ds(pl.multiple_of(half * part, part), part)]
        acc[:, :cols] += jnp.dot(a, wk[...], preferred_element_type=jnp.float32)
        acc[:, cols:] += jnp.dot(a, wv[...], preferred_element_type=jnp.float32)


def far_kernel(sizes, info, *refs):
    n = len(sizes)
    slabs = refs[:n]
    joined_k, joined_v, came_k, came_v, joined, beside_k, beside_v = refs[n : n + 7]
    out, acts, held, act_sems, sems = refs[n + 7 :]
    starts = [sum(sizes[:c]) for c in range(n)]
    rows, cols = held.shape[1:]
    share = rows // 2
    weights = (joined_k, came_k, joined.at[pl.ds(0, rows)], beside_k)
    weights += (joined_v, came_v, joined.at[pl.ds(rows, rows)], beside_v)
    y, x, core = info[5], info[6], info[7]

    @pl.when(info[4] == 1)
    def _():
        loads = [
            pltpu.make_async_copy(
                slabs[c].at[pl.ds(s * sizes[c], sizes[c])], acts.at[s, pl.ds(starts[c], sizes[c])], act_sems.at[s, c]
            )
            for c in range(n)
            for s in range(2)
        ]
        copies = [pltpu.make_async_copy(w, held.at[i], sems.at[i]) for i, w in enumerate(weights)]
        for c in loads + copies:
            c.start()
        for c in loads:
            c.wait()
        for g in range(2):
            total = None
            for i in range(4):
                copies[4 * g + i].wait()
                here = core if i < 2 else 1 - core
                for t in range(2):
                    if g == 0:
                        slab, chip = t, (x if i % 2 == 0 else 1 - x)
                    else:
                        slab, chip = (y if i % 2 == 0 else 1 - y), t
                    at = pl.multiple_of((2 * chip + here) * share, 128)
                    a = acts[slab, :, pl.ds(at, share)]
                    w = held[4 * g + i, t * share : (t + 1) * share, :]
                    term = jnp.dot(a, w, preferred_element_type=jnp.float32)
                    total = term if total is None else total + term
            out[:, g * cols : (g + 1) * cols] = total.astype(jnp.bfloat16)


def finish_kernel(segments, whole, chained, plan, *refs):
    given = []
    at = 0
    for s in segments:
        n = len(s.accs) + len(s.parts)
        given.append(refs[at : at + n])
        at += n
    ssq_a, ssq_b, bk, bv, cosine, sine = refs[at : at + 6]
    refs = refs[at + 6 + (2 if chained else 0) :]
    k_out, v_out, acc_held, far_held, k_held, v_held, cos_held, sin_held, in_sems, rope_sems, out_sems = refs
    cols = k_held.shape[1]
    loads, spots = [], []
    for i, (s, arrays) in enumerate(zip(segments, given)):
        rows, here, count = s.rows, s.here, 2 * s.rows
        mine = [
            pltpu.make_async_copy(ref.at[pl.ds(row, count)], acc_held.at[t, pl.ds(here, count)], in_sems.at[i, t])
            for t, (row, ref) in enumerate(zip(s.accs, arrays))
        ]
        for p, ((row, col, wide), ref) in enumerate(zip(s.parts, arrays[len(s.accs) :])):
            mine.append(
                pltpu.make_async_copy(
                    ref.at[pl.ds(row, count)],
                    far_held.at[pl.ds(here, count), pl.ds(col, wide)],
                    in_sems.at[i, 2 + p],
                )
            )
        spots.append([pl.multiple_of(plan[s.first + j, 2] * BLOCK + s.low, 16) for j in range(2)])
        for j in range(2):
            for t, (src, dst) in enumerate(((cosine, cos_held), (sine, sin_held))):
                mine.append(
                    pltpu.make_async_copy(
                        src.at[pl.ds(spots[i][j], rows)], dst.at[pl.ds(here + j * rows, rows)], rope_sems.at[i, j, t]
                    )
                )
        for c in mine:
            c.start()
        loads.append(mine)
    stores = []
    for i, s in enumerate(segments):
        rows = s.rows
        for c in loads[i]:
            c.wait()
        for j in range(2):
            row = s.ssq + j
            sums = jnp.broadcast_to(ssq_a[row : row + 1, :] + ssq_b[row : row + 1, :], (8, BLOCK))
            scale = lax.rsqrt(sums.T[:rows, :1] * (1.0 / whole) + EPS)
            span = slice(s.here + j * rows, s.here + (j + 1) * rows)
            cos_rows, sin_rows = cos_held[span, :], sin_held[span, :]
            for h in range(cols // HD):
                lanes = slice(h * HD, (h + 1) * HD)
                k = acc_held[0, span, lanes]
                if len(s.accs) > 1:
                    k += acc_held[1, span, lanes]
                if s.parts:
                    k += far_held[span, lanes].astype(jnp.float32)
                k = k * scale + bk[:, lanes]
                k_held[span, lanes] = (k * cos_rows + pltpu.roll(k, HD // 2, 1) * sin_rows).astype(jnp.bfloat16)
                lanes_v = slice(cols + h * HD, cols + (h + 1) * HD)
                v = acc_held[0, span, lanes_v]
                if len(s.accs) > 1:
                    v += acc_held[1, span, lanes_v]
                if s.parts:
                    v += far_held[span, lanes_v].astype(jnp.float32)
                v_held[span, lanes] = (v * scale + bv[:, lanes]).astype(jnp.bfloat16)
            for t, (held, out) in enumerate(((k_held, k_out), (v_held, v_out))):
                stores.append(
                    pltpu.make_async_copy(
                        held.at[pl.ds(s.here + j * rows, rows)],
                        out.at[pl.ds(spots[i][j], rows)],
                        out_sems.at[i, j, t],
                    )
                )
                stores[-1].start()
    for c in stores:
        c.wait()


Segment = collections.namedtuple(
    "Segment", ("low", "rows", "first", "accs", "here", "ssq", "parts")
)


def grouped(cached_rows, counts, dest_table, positions, norm_gain, key_weight, value_weight, key_bias, value_bias):
    stores = lax.axis_size("store")
    z, y = lax.axis_index("tensor"), lax.axis_index("groups")
    tokens = positions.shape[0]
    per_row = tokens // BLOCK
    most = dest_table.shape[1] // stores
    cached = cached_rows[0]
    width = cached.shape[1]
    whole, cols = key_weight.shape
    part, share = width // 2, whole // 16
    dma = pltpu.SemaphoreType.DMA
    bf16 = functools.partial(jax.ShapeDtypeStruct, dtype=jnp.bfloat16)
    f32 = functools.partial(jax.ShapeDtypeStruct, dtype=jnp.float32)
    swap = {m: ("store", [(s, s ^ m) for s in range(stores)]) for m in range(1, stores)}
    pair = ("tensor", [(0, 1), (1, 0), (2, 3), (3, 2)])
    middle = ("tensor", [(1, 2), (2, 1)])
    inward = ("tensor", [(0, 1), (3, 2)])
    outward = ("tensor", [(1, 0), (2, 3)])
    across = ("groups", [(0, 1), (1, 0)])
    ends = ("tensor", [(0, 3), (1, 2), (2, 1), (3, 0)])

    inner = (z == 1) | (z == 2)
    other = [jnp.where(inner, 3 - z, z ^ 2), jnp.where(inner, (3 - z) ^ 1, 3 - z)]
    chip, core = lax.axis_index("store") // 2, lax.rem(lax.axis_index("store"), 2)
    info = jnp.stack([z, z ^ 1, *other, inner.astype(jnp.int32), y, chip, core]).astype(jnp.int32)
    gain = lax.dynamic_slice_in_dim(norm_gain, z * width, width, 0)[None, :]
    cosine, sine = rope_tables(positions)

    call = Chain()
    came, own, ssq, ex, mr, fw, accs, far = {}, {}, {}, {}, {}, {}, {}, {}
    done = []

    def move(label, array, way):
        with jax.named_scope(label):
            return lax.ppermute(array, *way)

    def send(*parts):
        shapes = [bf16((sum(s[2] for _, _, s in p), width)) for p in parts]
        return call(
            functools.partial(send_kernel, parts, per_row),
            "send",
            (dest_table, cached),
            [SMEM, HBM],
            shapes,
            [VMEM] * len(shapes),
            [dma((sum(len(p) for p in parts),))],
        )

    def prep(c):
        k, low, rows = CHUNKS[c]
        pieces, arrays = [], []
        for r in range(k + 1):
            pieces.append((r, 1, 0, BLOCK, r * BLOCK))
            arrays.append(beside)
        for i, (r, p_low, p_rows) in enumerate(STEPS):
            if r <= k and p_low < low + rows and low < p_low + p_rows:
                for m in (2, 3):
                    array, at = came[i][m]
                    pieces.append((r, m, p_low, p_rows, at))
                    arrays.append(array)
        own[c], ssq[c] = call(
            functools.partial(prep_kernel, low, rows, 2 * k, stores, pieces),
            "prep",
            (plan, cached, *arrays, gain),
            [SMEM, HBM] + [HBM] * len(pieces) + [VMEM],
            [bf16((2 * rows, width)), f32((2, BLOCK))],
            [VMEM, VMEM],
            [pltpu.VMEM((2, rows, width), jnp.bfloat16), dma((2,))],
        )

    def pass_own(c):
        ex[c] = move("ex%d" % c, own[c], pair)

    def relay(c):
        rows = 2 * CHUNKS[c][2]
        (both,) = call(
            relay_kernel, "relay", (own[c], ex[c]), [HBM] * 2, [bf16((2 * rows, width))], [VMEM], [dma((2,))]
        )
        mr[c] = move("mr%d" % c, both, middle)

    def pin(*arrays, cost=COST):
        return call.pin("pin", arrays, cost)

    def hand(c):
        fw[c] = move("fw%d" % c, mr[c], outward)

    def sums(step, *arrays):
        (out,) = call(
            functools.partial(sums_kernel, step), "sums", arrays, [VMEM] * len(arrays), [f32((16, BLOCK))], [VMEM]
        )
        return out

    def near(taken, first, last, handed):
        sizes = [2 * CHUNKS[c][2] for c in taken]
        total = sum(sizes)
        kinds = ((own, ex) if first == 0 else ()) + ((mr,) if last == 4 else ()) + ((fw,) if last == 4 and handed else ())
        slabs = [kind[c] for c in taken for kind in kinds]

        def weights(i, info):
            slab = first + i // 2
            skip = (slab >= 2) & (info[4] == 0) & (not handed)
            return (jnp.where(skip, info[1] * 2 + 1, info[slab] * 2 + lax.rem(i, 2)), 0)

        (acc,) = call(
            functools.partial(near_kernel, sizes, first, handed),
            "near",
            (info, *slabs, key_weight, value_weight),
            [HBM] * len(slabs) + [pl.BlockSpec((part, cols), weights)] * 2,
            [f32((total, 2 * cols))],
            [pl.BlockSpec((total, 2 * cols), lambda i, info: (0, 0))],
            [pltpu.VMEM((last - first, total, width), jnp.bfloat16), dma((last - first, len(sizes)))],
            grid=(2 * (last - first),),
        )
        for i, c in enumerate(taken):
            accs.setdefault(c, []).append((acc, sum(sizes[:i])))

    def reach(*taken):
        sizes = [2 * CHUNKS[c][2] for c in taken]
        total = sum(sizes)
        (out,) = call(
            functools.partial(far_kernel, sizes),
            "far",
            (info, *(mr[c] for c in taken), *reached),
            [SMEM] + [HBM] * (len(taken) + len(reached)),
            [bf16((total, 2 * cols))],
            [VMEM],
            [
                pltpu.VMEM((2, total, width), jnp.bfloat16),
                pltpu.VMEM((8, *reached[0].shape), jnp.bfloat16),
                dma((2, len(sizes))),
                dma((8,)),
            ],
        )
        out = move("far%d" % taken[0], out, outward)
        for i, c in enumerate(taken):
            far.setdefault(c, []).append((out, (sum(sizes[:i]), 0, 2 * cols)))

    def finish(*taken):
        segments, arrays, here = [], [], 0
        for c in taken:
            k, low, rows = CHUNKS[c]
            arrays += [a for a, _ in accs[c]] + [a for a, _ in far.get(c, [])]
            segments.append(
                Segment(low, rows, 2 * k, [r for _, r in accs[c]], here, 2 * c, [p for _, p in far.get(c, [])])
            )
            here += 2 * rows
        most_accs = max(len(s.accs) for s in segments)
        args = [plan, *arrays, *total_squares, key_bias[None, :], value_bias[None, :], cosine, sine, *done]
        done[:] = call(
            functools.partial(finish_kernel, segments, whole, bool(done)),
            "finish",
            tuple(args),
            [SMEM] + [HBM] * len(arrays) + [VMEM] * 4 + [HBM] * (2 + len(done)),
            [bf16((tokens, cols))] * 2,
            [HBM] * 2,
            [
                pltpu.VMEM((most_accs, here, 2 * cols), jnp.float32),
                pltpu.VMEM((here, 2 * cols), jnp.bfloat16),
                pltpu.VMEM((here, cols), jnp.bfloat16),
                pltpu.VMEM((here, cols), jnp.bfloat16),
                pltpu.VMEM((here, HD), jnp.float32),
                pltpu.VMEM((here, HD), jnp.float32),
                dma((len(segments), 4)),
                dma((len(segments), 2, 2)),
                dma((len(segments), 2, 2)),
            ],
            aliases={len(args) - 2: 0, len(args) - 1: 1} if done else None,
        )

    def both_ways(i):
        return [[(0, m, STEPS[i])] for m in (2, 3)]

    def exchange(i, sent):
        came[i] = {m: (move("a%d" % i, array, swap[m]), 0) for m, array in zip((2, 3), sent)}

    tables = [move("table", dest_table, swap[m]) for m in range(1, stores)]
    *s0, bulk = send(*both_ways(0), [(k * BLOCK, 1, (k, 0, BLOCK)) for k in range(most)])
    exchange(0, s0)
    beside = move("beside", bulk, swap[1])
    (plan,) = call(
        functools.partial(plan_kernel, stores, per_row),
        "plan",
        (dest_table, *tables),
        [SMEM] * stores,
        [jax.ShapeDtypeStruct((per_row, 4), jnp.int32)],
        [SMEM],
    )
    (lent,) = call(
        cut_kernel, "cut", (key_weight, value_weight), [HBM] * 2, [bf16((2 * share, cols))], [VMEM], [dma((2,))]
    )
    both = [[(m % 2 * 2 * BLOCK + t * BLOCK, m, STEPS[3 + t]) for m in (2, 3) for t in range(2)]]
    *s1, s2a, s2b, s3 = send(*both_ways(1), *both_ways(2), *both)
    exchange(1, s1)
    prep(0)
    pass_own(0)
    prep(1)
    pass_own(1)
    s2a, s2b, lent = pin(s2a, s2b, lent)
    exchange(2, (s2a, s2b))
    lent = move("in", lent, inward)
    relay(0)
    relay(1)
    prep(2)
    pass_own(2)
    (s3,) = pin(s3)
    late = move("h3", s3, swap[2])
    (mr[0],) = pin(mr[0])
    hand(0)
    near((0, 1), 0, 2, True)
    mr[1], fw[0], lent = pin(mr[1], fw[0], lent)
    hand(1)
    relay(2)
    (late,) = pin(late)
    turned = move("c3", late, swap[1])
    for t in range(2):
        came[3 + t] = {2: (late, t * BLOCK), 3: (turned, 2 * BLOCK + t * BLOCK)}
    lent_k, lent_v = call(
        split_kernel, "split", (lent,), [HBM], [bf16((share, cols))] * 2, [VMEM] * 2, [dma((2,))]
    )
    came_k, came_v = move("wk1", lent_k, across), move("wv1", lent_v, swap[2])
    prep(3)
    pass_own(3)
    prep(4)
    (fw[1],) = pin(fw[1])
    squares = sums(0, *(ssq[c] for c in range(len(CHUNKS))))
    paired = move("half", squares, pair)
    joined_k, joined_v, joined = call(
        join_kernel,
        "join",
        (info, lent_k, came_k, lent_v, came_v),
        [SMEM] + [HBM] * 4,
        [bf16((2 * share, cols))] * 2 + [bf16((4 * share, cols))],
        [VMEM] * 3,
        [dma((2, 2, 2))],
    )
    came_k, came_v = move("wk2", joined_k, swap[2]), move("wv2", joined_v, across)
    near((0, 1), 2, 4, True)
    squares = sums(1, squares, paired)
    rest = move("rest", squares, ends)
    relay(3)
    (own[4],) = pin(own[4])
    pass_own(4)
    mr[2], rest = pin(mr[2], rest)
    hand(2)
    total_squares = (squares, rest)
    near((2, 3), 0, 2, True)
    finish(0, 1)
    came_k, came_v, joined = pin(came_k, came_v, joined)
    beside_w = [move("core", w, swap[1]) for w in (joined, came_k, came_v)]
    near((4,), 0, 2, True)
    (mr[3],) = pin(mr[3])
    relay(4)
    (fw[2],) = pin(fw[2], cost=FAR)
    reached = (joined_k, joined_v, came_k, came_v, *beside_w)
    reach(3)
    near((2,), 2, 4, True)
    finish(2)
    reach(4)
    near((3, 4), 2, 4, False)
    finish(3)
    finish(4)
    return tuple(done)


def slot_ranks(dest_table, counts, per_row):
    slot_ids = jnp.arange(dest_table.shape[1], dtype=jnp.int32)
    is_valid = slot_ids[None, :] < counts[:, None]
    row_ids = jnp.where(is_valid, dest_table // per_row, -1)
    earlier = (
        (row_ids[:, :, None] == row_ids[:, None, :])
        & (slot_ids[None, None, :] < slot_ids[None, :, None])
        & is_valid[:, None, :]
    )
    return is_valid, row_ids, jnp.sum(earlier.astype(jnp.int32), axis=2)


def rotate_keys(key_raw, positions):
    rows, cols = key_raw.shape
    cosine, sine = rope_tables(positions)
    heads = key_raw.reshape(rows, cols // HD, HD)
    turned = heads * cosine[:, None, :] + jnp.roll(heads, HD // 2, axis=2) * sine[:, None, :]
    return turned.reshape(rows, cols)


def gathered(cached_rows, counts, dest_table, positions, norm_gain, key_weight, value_weight, key_bias, value_bias):
    stores = lax.axis_size("store")
    own_row = lax.axis_index("store")
    capacity = dest_table.shape[1]
    per_pair = capacity // stores
    per_row = positions.shape[0] // BLOCK
    width = cached_rows.shape[2]
    flat_slots = cached_rows.reshape(capacity, BLOCK * width)
    all_counts = lax.all_gather(counts, "store", axis=0, tiled=True)
    all_table = lax.all_gather(dest_table, "store", axis=0, tiled=True)
    is_valid, _, row_rank = slot_ranks(all_table, all_counts, per_row)
    target = own_row * per_row + jnp.arange(per_row, dtype=jnp.int32)
    own_valid, own_rows, own_rank = slot_ranks(dest_table, counts, per_row)
    pick = (
        own_valid[0][None, None, :]
        & (own_rows[0][None, None, :] == jnp.arange(stores, dtype=jnp.int32)[:, None, None])
        & (own_rank[0][None, None, :] == jnp.arange(per_pair, dtype=jnp.int32)[None, :, None])
    ).astype(jnp.bfloat16)
    outgoing = jnp.einsum("rkj,jf->rkf", pick, flat_slots, preferred_element_type=jnp.float32)
    arrived = lax.all_to_all(outgoing.astype(jnp.bfloat16), "store", split_axis=0, concat_axis=0, tiled=True)
    placing = (
        is_valid[None, :, :, None]
        & (all_table[None, :, :, None] == target[:, None, None, None])
        & (row_rank[None, :, :, None] == jnp.arange(per_pair, dtype=jnp.int32)[None, None, None, :])
    )
    placing = jnp.sum(placing.astype(jnp.int32), axis=2).astype(jnp.bfloat16)
    local = jnp.einsum("bsk,skf->bf", placing, arrived, preferred_element_type=jnp.float32)
    local = local.astype(jnp.bfloat16).reshape(per_row * BLOCK, width)
    rows = lax.all_gather(local, "tensor", axis=1, tiled=True).astype(jnp.float32)
    scale = lax.rsqrt(jnp.mean(rows * rows, axis=1) + EPS)
    normed = (rows * scale[:, None] * norm_gain[None, :]).astype(jnp.bfloat16)
    keys = jnp.dot(normed, key_weight, preferred_element_type=jnp.float32) + key_bias[None, :]
    values = jnp.dot(normed, value_weight, preferred_element_type=jnp.float32) + value_bias[None, :]
    return rotate_keys(keys, positions).astype(jnp.bfloat16), values.astype(jnp.bfloat16)


def solution(mesh):
    in_specs = (
        P(("groups", "store"), None, "tensor"),
        P(("groups", "store")),
        P(("groups", "store"), None),
        P(("groups", "store")),
        P(),
        P(None, "tensor"),
        P(None, "tensor"),
        P("tensor"),
        P("tensor"),
    )
    out_specs = (P(("groups", "store"), "tensor"), P(("groups", "store"), "tensor"))
    small = tuple(mesh.shape[axis] for axis in ("groups", "store", "tensor")) == (2, 4, 4)
    body = grouped if small else gathered
    return jax.shard_map(body, mesh=mesh, in_specs=in_specs, out_specs=out_specs, check_vma=False)
```

```python
import collections
import functools

import jax
import jax.numpy as jnp
from jax import lax
from jax.experimental import pallas as pl
from jax.experimental.pallas import tpu as pltpu
from jax.sharding import PartitionSpec as P

HD = 128
BLOCK = 128
ROPE_BASE = 1000000.0
EPS = 1e-06
MIB = 1 << 20
VMEM_LIMIT = 63 * MIB
COST = 4 * 10**9
FAR = 10**11
HBM = pl.BlockSpec(memory_space=pltpu.HBM)
SMEM = pl.BlockSpec(memory_space=pltpu.SMEM)
VMEM = pl.BlockSpec(memory_space=pltpu.VMEM)
TOKEN = jax.ShapeDtypeStruct((8, 128), jnp.int32)

STEPS = ((0, 0, 64), (0, 64, 64), (1, 0, 128), (2, 0, 128), (3, 0, 128))
CHUNKS = ((0, 0, 64), (0, 64, 64), (1, 0, 128), (2, 0, 128), (3, 0, 128))


def rope_tables(positions):
    half = HD // 2
    inverse = 1.0 / ROPE_BASE ** (jnp.arange(half, dtype=jnp.float32) * 2.0 / HD)
    angles = positions.astype(jnp.float32)[:, None] * inverse[None, :]
    cosine, sine = jnp.cos(angles), jnp.sin(angles)
    return (
        jnp.concatenate([cosine, cosine], axis=1),
        jnp.concatenate([-sine, sine], axis=1),
    )


class Chain:
    def __init__(self):
        self.token = None

    def __call__(self, kernel, name, args, specs, outs, out_specs, scratch=(), grid=None, aliases=None, cost=COST):
        first = self.token is None
        prefetch = 0 if grid is None else 1
        taken, given = len(args), len(outs)

        def body(*refs):
            ins = refs[:taken]
            after = taken + (0 if first else 1)
            kernel(*ins, *refs[after : after + given], *refs[after + given + 1 :])

        tokens = () if first else (self.token,)
        in_specs = list(specs) + [HBM] * len(tokens)
        out_specs = list(out_specs) + [HBM]
        if grid is None:
            where = dict(in_specs=in_specs, out_specs=out_specs, scratch_shapes=list(scratch))
        else:
            where = dict(
                grid_spec=pltpu.PrefetchScalarGridSpec(
                    num_scalar_prefetch=prefetch,
                    grid=grid,
                    in_specs=in_specs,
                    out_specs=out_specs,
                    scratch_shapes=list(scratch),
                )
            )
        result = pl.pallas_call(
            body,
            out_shape=tuple(outs) + (TOKEN,),
            input_output_aliases=aliases or {},
            compiler_params=pltpu.CompilerParams(vmem_limit_bytes=VMEM_LIMIT),
            cost_estimate=pl.CostEstimate(flops=cost, bytes_accessed=1, transcendentals=0),
            name=name,
            **where,
        )(*args, *tokens)
        self.token = result[-1]
        return result[:-1]

    def pin(self, name, arrays, cost=COST):
        outs = [jax.ShapeDtypeStruct(a.shape, a.dtype) for a in arrays]
        n = len(arrays)
        return self(
            lambda *refs: None, name, arrays, [HBM] * n, outs, [HBM] * n, aliases={i: i for i in range(n)}, cost=cost
        )


def in_row(table, low, per_row):
    start, count = jnp.int32(0), jnp.int32(0)
    for s in range(table.shape[1]):
        block = table[0, s]
        start += ((block >= 0) & (block < low)).astype(jnp.int32)
        count += ((block >= low) & (block < low + per_row)).astype(jnp.int32)
    return start, count


def plan_kernel(stores, per_row, *refs):
    tables, plan = refs[:-1], refs[-1]
    low = lax.axis_index("store") * per_row
    spans = [in_row(t, low, per_row) for t in tables]
    n = jnp.int32(0)
    for i in range(per_row):
        for f in range(3):
            plan[i, f] = jnp.int32(0)
    for r in range(tables[0].shape[1] // stores):
        for m in range(stores):
            start, count = spans[m]
            valid = r < count

            @pl.when(valid)
            def _():
                plan[n, 0] = jnp.int32(r * stores + m)
                plan[n, 1] = start + r
                plan[n, 2] = tables[m][0, start + r] - low

            n += valid.astype(jnp.int32)


def send_kernel(steps, per_row, table, cached, *refs):
    outs, sems = refs[:-1], refs[-1]
    own_row = lax.axis_index("store")
    last = table.shape[1] - 1
    starts = {m: in_row(table, (own_row ^ m) * per_row, per_row)[0] for m in {m for s in steps for _, m, _ in s}}
    copies = []
    for out, parts in zip(outs, steps):
        for at, m, (k, low, rows) in parts:
            src = pl.multiple_of(jnp.minimum(starts[m] + k, last) * BLOCK + low, 16)
            copies.append(
                pltpu.make_async_copy(cached.at[pl.ds(src, rows)], out.at[pl.ds(at, rows)], sems.at[len(copies)])
            )
            copies[-1].start()
    for c in copies:
        c.wait()


def pack_kernel(per_row, table, cached, passed, *refs):
    outs, sems = refs[:-1], refs[-1]
    start, _ = in_row(table, (lax.axis_index("store") ^ 2) * per_row, per_row)
    copies = []
    for i, out in enumerate(outs):
        src = pl.multiple_of(jnp.minimum(start + i + 1, table.shape[1] - 1) * BLOCK, 16)
        copies.append(pltpu.make_async_copy(cached.at[pl.ds(src, BLOCK)], out.at[pl.ds(0, BLOCK)], sems.at[i, 0]))
        here = passed.at[pl.ds(i * BLOCK, BLOCK)]
        copies.append(pltpu.make_async_copy(here, out.at[pl.ds(BLOCK, BLOCK)], sems.at[i, 1]))
    for c in copies:
        c.start()
    for c in copies:
        c.wait()


def cut_kernel(key_weight, value_weight, *refs):
    outs, sems = refs[:-1], refs[-1]
    z, y, own_row = lax.axis_index("tensor"), lax.axis_index("groups"), lax.axis_index("store")
    share = outs[0].shape[0]
    slab = jnp.where(z == 0, 2 + y, 1 - y)
    at = pl.multiple_of((slab * 4 + own_row) * share, 128)
    copies = [
        pltpu.make_async_copy(weight.at[pl.ds(at, share)], out, sems.at[g])
        for g, (weight, out) in enumerate(zip((key_weight, value_weight), outs))
    ]
    for c in copies:
        c.start()
    for c in copies:
        c.wait()


def join_kernel(axis, info, here, came, *refs):
    before, outs, sems = refs[:axis], refs[axis:-1], refs[-1]
    share = here.shape[0]
    place = info[5 + axis]
    copies = []
    for t, src in enumerate((here, came)):
        at = pl.multiple_of((place if t == 0 else 1 - place) * share, 128)
        copies.append(pltpu.make_async_copy(src, outs[0].at[pl.ds(at, share)], sems.at[0, t]))
        if axis == 1:
            copies.append(pltpu.make_async_copy(src, outs[1].at[pl.ds(at + 2 * share, share)], sems.at[1, t]))
    if axis == 1:
        copies.append(pltpu.make_async_copy(before[0], outs[1].at[pl.ds(0, 2 * share)], sems.at[2, 0]))
    for c in copies:
        c.start()
    for c in copies:
        c.wait()


def prep_kernel(low, rows, first, stores, pieces, plan, cached, *refs):
    arrived = refs[: len(pieces)]
    gain, y_out, ssq_out, held, sems = refs[len(pieces) :]
    width = held.shape[2]
    z = lax.axis_index("tensor")
    for j in range(2):
        code = plan[first + j, 0]

        @pl.when(lax.rem(code, stores) == 0)
        def _():
            start = pl.multiple_of(plan[first + j, 1] * BLOCK + low, 16)
            pltpu.make_async_copy(cached.at[pl.ds(start, rows)], held.at[j], sems.at[j]).start()

        for (r, m, p_low, p_rows, at), ref in zip(pieces, arrived):
            a, b = max(low, p_low), min(low + rows, p_low + p_rows)

            @pl.when(code == r * stores + m)
            def _():
                pltpu.make_async_copy(
                    ref.at[pl.ds(at + a - p_low, b - a)], held.at[j, pl.ds(a - low, b - a)], sems.at[j]
                ).start()

    for j in range(2):
        pltpu.make_async_copy(cached.at[pl.ds(0, rows)], held.at[j], sems.at[j]).wait()
        sums = jnp.zeros((rows, 128), jnp.float32)
        for c in range(0, width, 128):
            x = held[j, :, c : c + 128].astype(jnp.float32)
            here = gain[:, pl.ds(pl.multiple_of(z * width + c, 128), 128)]
            y_out[j * rows : (j + 1) * rows, c : c + 128] = (x * here).astype(jnp.bfloat16)
            sums += x * x
        ssq_out[j : j + 1, :rows] = jnp.sum(sums.T, axis=0, keepdims=True)


def sums_kernel(step, *refs):
    out = refs[-1]
    if step == 0:
        out[...] = jnp.zeros_like(out)
        for i, ref in enumerate(refs[:-1]):
            out[2 * i : 2 * i + 2, :] = ref[...]
    else:
        out[...] = refs[0][...] + refs[1][...]


def relay_kernel(own, ex, out, sems):
    rows = own.shape[0]
    copies = [
        pltpu.make_async_copy(src, out.at[pl.ds(i * rows, rows)], sems.at[i]) for i, src in enumerate((own, ex))
    ]
    for c in copies:
        c.start()
    for c in copies:
        c.wait()


def near_kernel(sizes, first, handed, info, *refs):
    n = len(sizes)
    wk, wv, acc, acts, sems = refs[-5:]
    arrays = refs[:-5]
    per = len(arrays) // n
    slabs = acts.shape[0]
    i = pl.program_id(0)
    slab, half = first + i // 2, lax.rem(i, 2)
    inner = info[4] == 1
    full = (i >= 0) if handed else inner
    starts = [sum(sizes[:c]) for c in range(n)]

    def copies(s, which, skip=0):
        return [
            pltpu.make_async_copy(
                arrays[per * c + which].at[pl.ds(skip * sizes[c], sizes[c])],
                acts.at[s - first, pl.ds(starts[c], sizes[c])],
                sems.at[s - first, c],
            )
            for c in range(n)
        ]

    @pl.when(i == 0)
    def _():
        for s in range(first, first + slabs):
            if s < 2:
                for c in copies(s, s):
                    c.start()
            else:

                @pl.when(inner)
                def _():
                    for c in copies(s, 2 - first, s - 2):
                        c.start()

                if handed:

                    @pl.when(jnp.logical_not(inner))
                    def _():
                        for c in copies(s, 3 - first, s - 2):
                            c.start()

    for s in range(first, first + slabs):

        @pl.when((half == 0) & (slab == s) & ((s < 2) | full))
        def _():
            for c in copies(s, 0):
                c.wait()

    part, cols = wk.shape

    @pl.when(i == 0)
    def _():
        if first >= 2 and not handed:
            acc[...] = jnp.zeros_like(acc)

        @pl.when((first < 2) | full)
        def _():
            a = acts[0, :, :part]
            acc[:, :cols] = jnp.dot(a, wk[...], preferred_element_type=jnp.float32)
            acc[:, cols:] = jnp.dot(a, wv[...], preferred_element_type=jnp.float32)

    @pl.when((i > 0) & ((slab < 2) | full))
    def _():
        a = acts[slab - first, :, pl.ds(pl.multiple_of(half * part, part), part)]
        acc[:, :cols] += jnp.dot(a, wk[...], preferred_element_type=jnp.float32)
        acc[:, cols:] += jnp.dot(a, wv[...], preferred_element_type=jnp.float32)


def far_kernel(sizes, info, *refs):
    n = len(sizes)
    slabs = refs[:n]
    joined_k, joined_v, came_k, came_v, joined, beside_k, beside_v = refs[n : n + 7]
    out, acts, held, act_sems, sems = refs[n + 7 :]
    starts = [sum(sizes[:c]) for c in range(n)]
    rows, cols = held.shape[1:]
    share = rows // 2
    weights = (joined_k, came_k, joined.at[pl.ds(0, rows)], beside_k)
    weights += (joined_v, came_v, joined.at[pl.ds(rows, rows)], beside_v)
    y, x, core = info[5], info[6], info[7]

    @pl.when(info[4] == 1)
    def _():
        loads = [
            pltpu.make_async_copy(
                slabs[c].at[pl.ds(s * sizes[c], sizes[c])], acts.at[s, pl.ds(starts[c], sizes[c])], act_sems.at[s, c]
            )
            for c in range(n)
            for s in range(2)
        ]
        copies = [pltpu.make_async_copy(w, held.at[i], sems.at[i]) for i, w in enumerate(weights)]
        for c in loads + copies:
            c.start()
        for c in loads:
            c.wait()
        for g in range(2):
            total = None
            for i in range(4):
                copies[4 * g + i].wait()
                here = core if i < 2 else 1 - core
                for t in range(2):
                    if g == 0:
                        slab, chip = t, (x if i % 2 == 0 else 1 - x)
                    else:
                        slab, chip = (y if i % 2 == 0 else 1 - y), t
                    at = pl.multiple_of((2 * chip + here) * share, 128)
                    a = acts[slab, :, pl.ds(at, share)]
                    w = held[4 * g + i, t * share : (t + 1) * share, :]
                    term = jnp.dot(a, w, preferred_element_type=jnp.float32)
                    total = term if total is None else total + term
            out[:, g * cols : (g + 1) * cols] = total.astype(jnp.bfloat16)


def finish_kernel(segments, whole, chained, plan, *refs):
    given = []
    at = 0
    for s in segments:
        n = len(s.accs) + len(s.parts)
        given.append(refs[at : at + n])
        at += n
    ssq_a, ssq_b, bk, bv, cosine, sine = refs[at : at + 6]
    refs = refs[at + 6 + (2 if chained else 0) :]
    k_out, v_out, acc_held, far_held, k_held, v_held, cos_held, sin_held, in_sems, rope_sems, out_sems = refs
    cols = k_held.shape[1]
    loads, spots = [], []
    for i, (s, arrays) in enumerate(zip(segments, given)):
        rows, here, count = s.rows, s.here, 2 * s.rows
        mine = [
            pltpu.make_async_copy(ref.at[pl.ds(row, count)], acc_held.at[t, pl.ds(here, count)], in_sems.at[i, t])
            for t, (row, ref) in enumerate(zip(s.accs, arrays))
        ]
        for p, ((row, col, wide), ref) in enumerate(zip(s.parts, arrays[len(s.accs) :])):
            mine.append(
                pltpu.make_async_copy(
                    ref.at[pl.ds(row, count)],
                    far_held.at[pl.ds(here, count), pl.ds(col, wide)],
                    in_sems.at[i, 2 + p],
                )
            )
        spots.append([pl.multiple_of(plan[s.first + j, 2] * BLOCK + s.low, 16) for j in range(2)])
        for j in range(2):
            for t, (src, dst) in enumerate(((cosine, cos_held), (sine, sin_held))):
                mine.append(
                    pltpu.make_async_copy(
                        src.at[pl.ds(spots[i][j], rows)], dst.at[pl.ds(here + j * rows, rows)], rope_sems.at[i, j, t]
                    )
                )
        for c in mine:
            c.start()
        loads.append(mine)
    stores = []
    for i, s in enumerate(segments):
        rows = s.rows
        for c in loads[i]:
            c.wait()
        for j in range(2):
            row = s.ssq + j
            sums = jnp.broadcast_to(ssq_a[row : row + 1, :] + ssq_b[row : row + 1, :], (8, BLOCK))
            scale = lax.rsqrt(sums.T[:rows, :1] * (1.0 / whole) + EPS)
            span = slice(s.here + j * rows, s.here + (j + 1) * rows)
            cos_rows, sin_rows = cos_held[span, :], sin_held[span, :]
            for h in range(cols // HD):
                lanes = slice(h * HD, (h + 1) * HD)
                k = acc_held[0, span, lanes]
                if len(s.accs) > 1:
                    k += acc_held[1, span, lanes]
                if s.parts:
                    k += far_held[span, lanes].astype(jnp.float32)
                k = k * scale + bk[:, lanes]
                k_held[span, lanes] = (k * cos_rows + pltpu.roll(k, HD // 2, 1) * sin_rows).astype(jnp.bfloat16)
                lanes_v = slice(cols + h * HD, cols + (h + 1) * HD)
                v = acc_held[0, span, lanes_v]
                if len(s.accs) > 1:
                    v += acc_held[1, span, lanes_v]
                if s.parts:
                    v += far_held[span, lanes_v].astype(jnp.float32)
                v_held[span, lanes] = (v * scale + bv[:, lanes]).astype(jnp.bfloat16)
            for t, (held, out) in enumerate(((k_held, k_out), (v_held, v_out))):
                stores.append(
                    pltpu.make_async_copy(
                        held.at[pl.ds(s.here + j * rows, rows)],
                        out.at[pl.ds(spots[i][j], rows)],
                        out_sems.at[i, j, t],
                    )
                )
                stores[-1].start()
    for c in stores:
        c.wait()


Segment = collections.namedtuple(
    "Segment", ("low", "rows", "first", "accs", "here", "ssq", "parts")
)


def grouped(cached_rows, counts, dest_table, positions, norm_gain, key_weight, value_weight, key_bias, value_bias):
    stores = lax.axis_size("store")
    z, y = lax.axis_index("tensor"), lax.axis_index("groups")
    tokens = positions.shape[0]
    per_row = tokens // BLOCK
    most = dest_table.shape[1] // stores
    cached = cached_rows[0]
    width = cached.shape[1]
    whole, cols = key_weight.shape
    share = whole // 16
    dma = pltpu.SemaphoreType.DMA
    bf16 = functools.partial(jax.ShapeDtypeStruct, dtype=jnp.bfloat16)
    f32 = functools.partial(jax.ShapeDtypeStruct, dtype=jnp.float32)
    swap = {m: ("store", [(s, s ^ m) for s in range(stores)]) for m in range(1, stores)}
    pair = ("tensor", [(0, 1), (1, 0), (2, 3), (3, 2)])
    middle = ("tensor", [(1, 2), (2, 1)])
    inward = ("tensor", [(0, 1), (3, 2)])
    outward = ("tensor", [(1, 0), (2, 3)])
    across = ("groups", [(0, 1), (1, 0)])
    ends = ("tensor", [(0, 3), (1, 2), (2, 1), (3, 0)])

    inner = (z == 1) | (z == 2)
    other = [jnp.where(inner, 3 - z, z ^ 2), jnp.where(inner, (3 - z) ^ 1, 3 - z)]
    chip, core = lax.axis_index("store") // 2, lax.rem(lax.axis_index("store"), 2)
    info = jnp.stack([z, z ^ 1, *other, inner.astype(jnp.int32), y, chip, core]).astype(jnp.int32)
    gain = norm_gain[None, :]

    call = Chain()
    came, own, ssq, ex, mr, fw, accs, far = {}, {}, {}, {}, {}, {}, {}, {}
    done = []

    def move(label, array, way):
        with jax.named_scope(label):
            return lax.ppermute(array, *way)

    def send(*parts):
        shapes = [bf16((sum(s[2] for _, _, s in p), width)) for p in parts]
        return call(
            functools.partial(send_kernel, parts, per_row),
            "send",
            (dest_table, cached),
            [SMEM, HBM],
            shapes,
            [VMEM] * len(shapes),
            [dma((sum(len(p) for p in parts),))],
        )

    def prep(c, cost=COST):
        k, low, rows = CHUNKS[c]
        pieces, arrays = [], []
        for r in range(k + 1):
            pieces.append((r, 1, 0, BLOCK, r * BLOCK))
            arrays.append(beside)
        for i, (r, p_low, p_rows) in enumerate(STEPS):
            if r <= k and p_low < low + rows and low < p_low + p_rows:
                for m in (2, 3):
                    array, at = came[i][m]
                    pieces.append((r, m, p_low, p_rows, at))
                    arrays.append(array)
        own[c], ssq[c] = call(
            functools.partial(prep_kernel, low, rows, 2 * k, stores, pieces),
            "prep",
            (plan, cached, *arrays, gain),
            [SMEM, HBM] + [HBM] * len(pieces) + [VMEM],
            [bf16((2 * rows, width)), f32((2, BLOCK))],
            [VMEM, VMEM],
            [pltpu.VMEM((2, rows, width), jnp.bfloat16), dma((2,))],
            cost=cost,
        )

    def pass_own(c):
        ex[c] = move("ex%d" % c, own[c], pair)

    def relay(c):
        rows = 2 * CHUNKS[c][2]
        (both,) = call(
            relay_kernel, "relay", (own[c], ex[c]), [HBM] * 2, [bf16((2 * rows, width))], [VMEM], [dma((2,))]
        )
        mr[c] = move("mr%d" % c, both, middle)

    def pin(*arrays, cost=COST):
        return call.pin("pin", arrays, cost)

    def hand(c):
        fw[c] = move("fw%d" % c, mr[c], outward)

    def sums(step, *arrays):
        (out,) = call(
            functools.partial(sums_kernel, step), "sums", arrays, [VMEM] * len(arrays), [f32((16, BLOCK))], [VMEM]
        )
        return out

    def near(taken, first, last, handed):
        sizes = [2 * CHUNKS[c][2] for c in taken]
        total = sum(sizes)
        kinds = ((own, ex) if first == 0 else ()) + ((mr,) if last == 4 else ()) + ((fw,) if last == 4 and handed else ())
        slabs = [kind[c] for c in taken for kind in kinds]

        def weights(i, info):
            slab = first + i // 2
            skip = (slab >= 2) & (info[4] == 0) & (not handed)
            return (jnp.where(skip, info[1] * 2 + 1, info[slab] * 2 + lax.rem(i, 2)), 0)

        (acc,) = call(
            functools.partial(near_kernel, sizes, first, handed),
            "near",
            (info, *slabs, key_weight, value_weight),
            [HBM] * len(slabs) + [pl.BlockSpec((width // 2, cols), weights)] * 2,
            [f32((total, 2 * cols))],
            [pl.BlockSpec((total, 2 * cols), lambda i, info: (0, 0))],
            [pltpu.VMEM((last - first, total, width), jnp.bfloat16), dma((last - first, len(sizes)))],
            grid=(2 * (last - first),),
        )
        for i, c in enumerate(taken):
            accs.setdefault(c, []).append((acc, sum(sizes[:i])))

    def reach(*taken):
        sizes = [2 * CHUNKS[c][2] for c in taken]
        total = sum(sizes)
        (out,) = call(
            functools.partial(far_kernel, sizes),
            "far",
            (info, *(mr[c] for c in taken), *reached),
            [SMEM] + [HBM] * (len(taken) + len(reached)),
            [bf16((total, 2 * cols))],
            [VMEM],
            [
                pltpu.VMEM((2, total, width), jnp.bfloat16),
                pltpu.VMEM((8, *reached[0].shape), jnp.bfloat16),
                dma((2, len(sizes))),
                dma((8,)),
            ],
        )
        out = move("far%d" % taken[0], out, outward)
        for i, c in enumerate(taken):
            far.setdefault(c, []).append((out, (sum(sizes[:i]), 0, 2 * cols)))

    def finish(*taken):
        segments, arrays, here = [], [], 0
        for c in taken:
            k, low, rows = CHUNKS[c]
            arrays += [a for a, _ in accs[c]] + [a for a, _ in far.get(c, [])]
            segments.append(
                Segment(low, rows, 2 * k, [r for _, r in accs[c]], here, 2 * c, [p for _, p in far.get(c, [])])
            )
            here += 2 * rows
        most_accs = max(len(s.accs) for s in segments)
        args = [plan, *arrays, *total_squares, key_bias[None, :], value_bias[None, :], cosine, sine, *done]
        done[:] = call(
            functools.partial(finish_kernel, segments, whole, bool(done)),
            "finish",
            tuple(args),
            [SMEM] + [HBM] * len(arrays) + [VMEM] * 4 + [HBM] * (2 + len(done)),
            [bf16((tokens, cols))] * 2,
            [HBM] * 2,
            [
                pltpu.VMEM((most_accs, here, 2 * cols), jnp.float32),
                pltpu.VMEM((here, 2 * cols), jnp.bfloat16),
                pltpu.VMEM((here, cols), jnp.bfloat16),
                pltpu.VMEM((here, cols), jnp.bfloat16),
                pltpu.VMEM((here, HD), jnp.float32),
                pltpu.VMEM((here, HD), jnp.float32),
                dma((len(segments), 4)),
                dma((len(segments), 2, 2)),
                dma((len(segments), 2, 2)),
            ],
            aliases={len(args) - 2: 0, len(args) - 1: 1} if done else None,
        )

    def both_ways(i):
        return [[(0, m, STEPS[i])] for m in (2, 3)]

    def exchange(i, sent):
        came[i] = {m: (move("a%d" % i, array, swap[m]), 0) for m, array in zip((2, 3), sent)}

    tables = [move("table", dest_table, swap[m]) for m in range(1, stores)]
    exchange(0, send(*both_ways(0)))
    (bulk,) = send([(k * BLOCK, 1, (k, 0, BLOCK)) for k in range(most)])
    beside = move("beside", bulk, swap[1])
    (plan,) = call(
        functools.partial(plan_kernel, stores, per_row),
        "plan",
        (dest_table, *tables),
        [SMEM] * stores,
        [jax.ShapeDtypeStruct((per_row, 4), jnp.int32)],
        [SMEM],
    )
    def join(axis, here, hopped, *before):
        return call(
            functools.partial(join_kernel, axis),
            "join",
            (info, here, hopped, *before),
            [SMEM] + [HBM] * (2 + axis),
            [bf16((2 * share, cols)), bf16((4 * share, cols))][: 1 + axis],
            [VMEM] * (1 + axis),
            [dma((3, 2))],
        )

    onward = [((k - 1) * BLOCK, 3, (k, 0, BLOCK)) for k in range(1, most)]
    *s1, passed = send(*both_ways(1), onward)
    exchange(1, s1)
    passed = move("pass", passed, swap[1])
    prep(0, FAR)
    pass_own(0)
    packs = call(
        functools.partial(pack_kernel, per_row),
        "pack",
        (dest_table, cached, passed),
        [SMEM, HBM, HBM],
        [bf16((2 * BLOCK, width))] * 3,
        [VMEM] * 3,
        [dma((3, 2))],
    )

    cuts = call(
        cut_kernel, "cut", (key_weight, value_weight), [HBM] * 2, [bf16((share, cols))] * 2, [VMEM] * 2, [dma((2,))]
    )

    def hop(k, pack):
        hopped = move("h%d" % k, pack, swap[2])
        came[k + 1] = {2: (hopped, 0), 3: (hopped, BLOCK)}

    prep(1)
    pass_own(1)
    pack, lent_k = pin(packs[0], cuts[0])
    hop(1, pack)
    lent_k = move("ink", lent_k, inward)
    relay(0)
    relay(1)
    prep(2)
    pass_own(2)
    (pack,) = pin(packs[1])
    hop(2, pack)
    (positions,) = pin(positions)
    cosine, sine = pin(*rope_tables(positions))
    mr[0], lent_k, lent_v = pin(mr[0], lent_k, cuts[1])
    hand(0)
    lent_v = move("inv", lent_v, inward)
    near((0, 1), 0, 2, True)
    relay(2)
    prep(3)
    pass_own(3)
    mr[1], pack = pin(mr[1], packs[2])
    hop(3, pack)
    fw[0], lent_v, lent_k, mr[1] = pin(fw[0], lent_v, lent_k, mr[1])
    hand(1)
    came_k = move("wk1", lent_k, across)
    (lent_v,) = pin(lent_v)
    came_v = move("wv1", lent_v, swap[2])
    near((2,), 0, 2, True)
    relay(3)
    (mr[2],) = pin(mr[2])
    prep(4)
    squares = sums(0, *(ssq[c] for c in range(len(CHUNKS))))
    paired = move("half", squares, pair)
    fw[1], own[4] = pin(fw[1], own[4])
    pass_own(4)
    (joined_k,) = join(0, lent_k, came_k)
    came_k = move("wk2", joined_k, swap[2])
    joined_v, joined = join(1, lent_v, came_v, joined_k)
    came_v = move("wv2", joined_v, across)
    mr[2], paired = pin(mr[2], paired)
    hand(2)
    near((3, 4), 0, 2, True)
    (mr[3],) = pin(mr[3])
    squares = sums(1, squares, paired)
    rest = move("rest", squares, ends)
    relay(4)
    near((0, 1), 2, 4, True)
    came_k, came_v, joined = pin(came_k, came_v, joined)
    beside_w = [move("core", w, swap[1]) for w in (joined, came_k, came_v)]
    total_squares = (squares, rest)
    finish(0, 1)
    (fw[2],) = pin(fw[2], cost=FAR)
    reached = (joined_k, joined_v, came_k, came_v, *beside_w)
    reach(3)
    near((2,), 2, 4, True)
    reach(4)
    near((3, 4), 2, 4, False)
    finish(2, 3)
    finish(4)
    return tuple(done)


def slot_ranks(dest_table, counts, per_row):
    slot_ids = jnp.arange(dest_table.shape[1], dtype=jnp.int32)
    is_valid = slot_ids[None, :] < counts[:, None]
    row_ids = jnp.where(is_valid, dest_table // per_row, -1)
    earlier = (
        (row_ids[:, :, None] == row_ids[:, None, :])
        & (slot_ids[None, None, :] < slot_ids[None, :, None])
        & is_valid[:, None, :]
    )
    return is_valid, row_ids, jnp.sum(earlier.astype(jnp.int32), axis=2)


def rotate_keys(key_raw, positions):
    rows, cols = key_raw.shape
    cosine, sine = rope_tables(positions)
    heads = key_raw.reshape(rows, cols // HD, HD)
    turned = heads * cosine[:, None, :] + jnp.roll(heads, HD // 2, axis=2) * sine[:, None, :]
    return turned.reshape(rows, cols)


def gathered(cached_rows, counts, dest_table, positions, norm_gain, key_weight, value_weight, key_bias, value_bias):
    stores = lax.axis_size("store")
    own_row = lax.axis_index("store")
    capacity = dest_table.shape[1]
    per_pair = capacity // stores
    per_row = positions.shape[0] // BLOCK
    width = cached_rows.shape[2]
    flat_slots = cached_rows.reshape(capacity, BLOCK * width)
    all_counts = lax.all_gather(counts, "store", axis=0, tiled=True)
    all_table = lax.all_gather(dest_table, "store", axis=0, tiled=True)
    is_valid, _, row_rank = slot_ranks(all_table, all_counts, per_row)
    target = own_row * per_row + jnp.arange(per_row, dtype=jnp.int32)
    own_valid, own_rows, own_rank = slot_ranks(dest_table, counts, per_row)
    pick = (
        own_valid[0][None, None, :]
        & (own_rows[0][None, None, :] == jnp.arange(stores, dtype=jnp.int32)[:, None, None])
        & (own_rank[0][None, None, :] == jnp.arange(per_pair, dtype=jnp.int32)[None, :, None])
    ).astype(jnp.bfloat16)
    outgoing = jnp.einsum("rkj,jf->rkf", pick, flat_slots, preferred_element_type=jnp.float32)
    arrived = lax.all_to_all(outgoing.astype(jnp.bfloat16), "store", split_axis=0, concat_axis=0, tiled=True)
    placing = (
        is_valid[None, :, :, None]
        & (all_table[None, :, :, None] == target[:, None, None, None])
        & (row_rank[None, :, :, None] == jnp.arange(per_pair, dtype=jnp.int32)[None, None, None, :])
    )
    placing = jnp.sum(placing.astype(jnp.int32), axis=2).astype(jnp.bfloat16)
    local = jnp.einsum("bsk,skf->bf", placing, arrived, preferred_element_type=jnp.float32)
    local = local.astype(jnp.bfloat16).reshape(per_row * BLOCK, width)
    rows = lax.all_gather(local, "tensor", axis=1, tiled=True).astype(jnp.float32)
    scale = lax.rsqrt(jnp.mean(rows * rows, axis=1) + EPS)
    normed = (rows * scale[:, None] * norm_gain[None, :]).astype(jnp.bfloat16)
    keys = jnp.dot(normed, key_weight, preferred_element_type=jnp.float32) + key_bias[None, :]
    values = jnp.dot(normed, value_weight, preferred_element_type=jnp.float32) + value_bias[None, :]
    return rotate_keys(keys, positions).astype(jnp.bfloat16), values.astype(jnp.bfloat16)


def solution(mesh):
    in_specs = (
        P(("groups", "store"), None, "tensor"),
        P(("groups", "store")),
        P(("groups", "store"), None),
        P(("groups", "store")),
        P(),
        P(None, "tensor"),
        P(None, "tensor"),
        P("tensor"),
        P("tensor"),
    )
    out_specs = (P(("groups", "store"), "tensor"), P(("groups", "store"), "tensor"))
    small = tuple(mesh.shape[axis] for axis in ("groups", "store", "tensor")) == (2, 4, 4)
    body = grouped if small else gathered
    return jax.shard_map(body, mesh=mesh, in_specs=in_specs, out_specs=out_specs, check_vma=False)
```

```python
import collections
import functools

import jax
import jax.numpy as jnp
from jax import lax
from jax.experimental import pallas as pl
from jax.experimental.pallas import tpu as pltpu
from jax.sharding import PartitionSpec as P

HD = 128
BLOCK = 128
ROPE_BASE = 1000000.0
EPS = 1e-06
MIB = 1 << 20
VMEM_LIMIT = 63 * MIB
COST = 4 * 10**9
FAR = 10**11
HBM = pl.BlockSpec(memory_space=pltpu.HBM)
SMEM = pl.BlockSpec(memory_space=pltpu.SMEM)
VMEM = pl.BlockSpec(memory_space=pltpu.VMEM)
TOKEN = jax.ShapeDtypeStruct((8, 128), jnp.int32)

STEPS = ((0, 0, 64), (0, 64, 64), (1, 0, 128), (2, 0, 128), (3, 0, 128))
CHUNKS = ((0, 0, 64), (0, 64, 64), (1, 0, 128), (2, 0, 128), (3, 0, 128))


def rope_tables(positions):
    half = HD // 2
    inverse = 1.0 / ROPE_BASE ** (jnp.arange(half, dtype=jnp.float32) * 2.0 / HD)
    angles = positions.astype(jnp.float32)[:, None] * inverse[None, :]
    cosine, sine = jnp.cos(angles), jnp.sin(angles)
    return (
        jnp.concatenate([cosine, cosine], axis=1),
        jnp.concatenate([-sine, sine], axis=1),
    )


class Chain:
    def __init__(self):
        self.token = None

    def __call__(self, kernel, name, args, specs, outs, out_specs, scratch=(), grid=None, aliases=None, cost=COST):
        first = self.token is None
        prefetch = 0 if grid is None else 1
        taken, given = len(args), len(outs)

        def body(*refs):
            ins = refs[:taken]
            after = taken + (0 if first else 1)
            kernel(*ins, *refs[after : after + given], *refs[after + given + 1 :])

        tokens = () if first else (self.token,)
        in_specs = list(specs) + [HBM] * len(tokens)
        out_specs = list(out_specs) + [HBM]
        if grid is None:
            where = dict(in_specs=in_specs, out_specs=out_specs, scratch_shapes=list(scratch))
        else:
            where = dict(
                grid_spec=pltpu.PrefetchScalarGridSpec(
                    num_scalar_prefetch=prefetch,
                    grid=grid,
                    in_specs=in_specs,
                    out_specs=out_specs,
                    scratch_shapes=list(scratch),
                )
            )
        result = pl.pallas_call(
            body,
            out_shape=tuple(outs) + (TOKEN,),
            input_output_aliases=aliases or {},
            compiler_params=pltpu.CompilerParams(vmem_limit_bytes=VMEM_LIMIT),
            cost_estimate=pl.CostEstimate(flops=cost, bytes_accessed=1, transcendentals=0),
            name=name,
            **where,
        )(*args, *tokens)
        self.token = result[-1]
        return result[:-1]

    def pin(self, name, arrays, cost=COST):
        outs = [jax.ShapeDtypeStruct(a.shape, a.dtype) for a in arrays]
        n = len(arrays)
        return self(
            lambda *refs: None, name, arrays, [HBM] * n, outs, [HBM] * n, aliases={i: i for i in range(n)}, cost=cost
        )


def in_row(table, low, per_row):
    start, count = jnp.int32(0), jnp.int32(0)
    for s in range(table.shape[1]):
        block = table[0, s]
        start += ((block >= 0) & (block < low)).astype(jnp.int32)
        count += ((block >= low) & (block < low + per_row)).astype(jnp.int32)
    return start, count


def plan_kernel(stores, per_row, *refs):
    tables, plan = refs[:-1], refs[-1]
    low = lax.axis_index("store") * per_row
    spans = [in_row(t, low, per_row) for t in tables]
    n = jnp.int32(0)
    for i in range(per_row):
        for f in range(3):
            plan[i, f] = jnp.int32(0)
    for r in range(tables[0].shape[1] // stores):
        for m in range(stores):
            start, count = spans[m]
            valid = r < count

            @pl.when(valid)
            def _():
                plan[n, 0] = jnp.int32(r * stores + m)
                plan[n, 1] = start + r
                plan[n, 2] = tables[m][0, start + r] - low

            n += valid.astype(jnp.int32)


def send_kernel(steps, per_row, table, cached, *refs):
    outs, sems = refs[:-1], refs[-1]
    own_row = lax.axis_index("store")
    last = table.shape[1] - 1
    starts = {m: in_row(table, (own_row ^ m) * per_row, per_row)[0] for m in {m for s in steps for _, m, _ in s}}
    copies = []
    for out, parts in zip(outs, steps):
        for at, m, (k, low, rows) in parts:
            src = pl.multiple_of(jnp.minimum(starts[m] + k, last) * BLOCK + low, 16)
            copies.append(
                pltpu.make_async_copy(cached.at[pl.ds(src, rows)], out.at[pl.ds(at, rows)], sems.at[len(copies)])
            )
            copies[-1].start()
    for c in copies:
        c.wait()


def pack_kernel(per_row, table, cached, passed, *refs):
    outs, sems = refs[:-1], refs[-1]
    start, _ = in_row(table, (lax.axis_index("store") ^ 2) * per_row, per_row)
    copies = []
    for i, out in enumerate(outs):
        src = pl.multiple_of(jnp.minimum(start + i + 1, table.shape[1] - 1) * BLOCK, 16)
        copies.append(pltpu.make_async_copy(cached.at[pl.ds(src, BLOCK)], out.at[pl.ds(0, BLOCK)], sems.at[i, 0]))
        here = passed.at[pl.ds(i * BLOCK, BLOCK)]
        copies.append(pltpu.make_async_copy(here, out.at[pl.ds(BLOCK, BLOCK)], sems.at[i, 1]))
    for c in copies:
        c.start()
    for c in copies:
        c.wait()


def cut_kernel(key_weight, value_weight, *refs):
    outs, sems = refs[:-1], refs[-1]
    z, y, own_row = lax.axis_index("tensor"), lax.axis_index("groups"), lax.axis_index("store")
    share = outs[0].shape[0]
    slab = jnp.where(z == 0, 2 + y, 1 - y)
    at = pl.multiple_of((slab * 4 + own_row) * share, 128)
    copies = [
        pltpu.make_async_copy(weight.at[pl.ds(at, share)], out, sems.at[g])
        for g, (weight, out) in enumerate(zip((key_weight, value_weight), outs))
    ]
    for c in copies:
        c.start()
    for c in copies:
        c.wait()


def join_kernel(axis, info, here, came, *refs):
    before, outs, sems = refs[:axis], refs[axis:-1], refs[-1]
    share = here.shape[0]
    place = info[5 + axis]
    copies = []
    for t, src in enumerate((here, came)):
        at = pl.multiple_of((place if t == 0 else 1 - place) * share, 128)
        copies.append(pltpu.make_async_copy(src, outs[0].at[pl.ds(at, share)], sems.at[0, t]))
        if axis == 1:
            copies.append(pltpu.make_async_copy(src, outs[1].at[pl.ds(at + 2 * share, share)], sems.at[1, t]))
    if axis == 1:
        copies.append(pltpu.make_async_copy(before[0], outs[1].at[pl.ds(0, 2 * share)], sems.at[2, 0]))
    for c in copies:
        c.start()
    for c in copies:
        c.wait()


def prep_kernel(low, rows, first, stores, pieces, plan, cached, *refs):
    arrived = refs[: len(pieces)]
    gain, y_out, ssq_out, held, sems = refs[len(pieces) :]
    width = held.shape[2]
    z = lax.axis_index("tensor")
    for j in range(2):
        code = plan[first + j, 0]

        @pl.when(lax.rem(code, stores) == 0)
        def _():
            start = pl.multiple_of(plan[first + j, 1] * BLOCK + low, 16)
            pltpu.make_async_copy(cached.at[pl.ds(start, rows)], held.at[j], sems.at[j]).start()

        for (r, m, p_low, p_rows, at), ref in zip(pieces, arrived):
            a, b = max(low, p_low), min(low + rows, p_low + p_rows)

            @pl.when(code == r * stores + m)
            def _():
                pltpu.make_async_copy(
                    ref.at[pl.ds(at + a - p_low, b - a)], held.at[j, pl.ds(a - low, b - a)], sems.at[j]
                ).start()

    for j in range(2):
        pltpu.make_async_copy(cached.at[pl.ds(0, rows)], held.at[j], sems.at[j]).wait()
        sums = jnp.zeros((rows, 128), jnp.float32)
        for c in range(0, width, 128):
            x = held[j, :, c : c + 128].astype(jnp.float32)
            here = gain[:, pl.ds(pl.multiple_of(z * width + c, 128), 128)]
            y_out[j * rows : (j + 1) * rows, c : c + 128] = (x * here).astype(jnp.bfloat16)
            sums += x * x
        ssq_out[j : j + 1, :rows] = jnp.sum(sums.T, axis=0, keepdims=True)


def sums_kernel(step, *refs):
    out = refs[-1]
    if step == 0:
        out[...] = jnp.zeros_like(out)
        for i, ref in enumerate(refs[:-1]):
            out[2 * i : 2 * i + 2, :] = ref[...]
    else:
        out[...] = refs[0][...] + refs[1][...]


def relay_kernel(own, ex, out, sems):
    rows = own.shape[0]
    copies = [
        pltpu.make_async_copy(src, out.at[pl.ds(i * rows, rows)], sems.at[i]) for i, src in enumerate((own, ex))
    ]
    for c in copies:
        c.start()
    for c in copies:
        c.wait()


def near_kernel(sizes, first, lead, counts, info, *refs):
    n = len(sizes)
    wk, wv, acc, acts, sems = refs[-5:]
    arrays = [refs[sum(counts[:c]) : sum(counts[: c + 1])] for c in range(n)]
    slabs = acts.shape[0]
    i = pl.program_id(0)
    slab, half = first + i // 2, lax.rem(i, 2)
    inner = info[4] == 1
    starts = [sum(sizes[:c]) for c in range(n)]

    def copies(s, which, skip=0, rows=sum(sizes)):
        return [
            pltpu.make_async_copy(
                arrays[c][which].at[pl.ds(skip * sizes[c], sizes[c])],
                acts.at[s - first, pl.ds(starts[c], sizes[c])],
                sems.at[s - first, c],
            )
            for c in range(n)
            if starts[c] < rows
        ]

    def held(s, fetch):
        if s < 2:
            fetch(copies(s, s))
        else:

            @pl.when(inner)
            def _():
                fetch(copies(s, 2 - first, s - 2))

            if lead:

                @pl.when(jnp.logical_not(inner))
                def _():
                    fetch(copies(s, 3 - first, s - 2, lead))

    def start(made):
        for c in made:
            c.start()

    def wait(made):
        for c in made:
            c.wait()

    @pl.when(i == 0)
    def _():
        for s in range(first, first + slabs):
            held(s, start)

    for s in range(first, first + slabs):

        @pl.when((half == 0) & (slab == s))
        def _():
            held(s, wait)

    part, cols = wk.shape

    @pl.when(i == 0)
    def _():
        acc[...] = jnp.zeros_like(acc)

    def add(rows):
        a = acts[slab - first, :rows, pl.ds(pl.multiple_of(half * part, part), part)]
        acc[:rows, :cols] += jnp.dot(a, wk[...], preferred_element_type=jnp.float32)
        acc[:rows, cols:] += jnp.dot(a, wv[...], preferred_element_type=jnp.float32)

    whole_rows = (slab < 2) | inner if lead < sum(sizes) else i >= 0

    @pl.when(whole_rows)
    def _():
        add(sum(sizes))

    if 0 < lead < sum(sizes):

        @pl.when(jnp.logical_not(whole_rows))
        def _():
            add(lead)


def far_kernel(sizes, info, *refs):
    n = len(sizes)
    slabs = refs[:n]
    joined_k, joined_v, came_k, came_v, joined, beside_k, beside_v = refs[n : n + 7]
    out, acts, held, act_sems, sems = refs[n + 7 :]
    starts = [sum(sizes[:c]) for c in range(n)]
    rows, cols = held.shape[1:]
    share = rows // 2
    weights = (joined_k, came_k, joined.at[pl.ds(0, rows)], beside_k)
    weights += (joined_v, came_v, joined.at[pl.ds(rows, rows)], beside_v)
    y, x, core = info[5], info[6], info[7]

    @pl.when(info[4] == 1)
    def _():
        loads = [
            pltpu.make_async_copy(
                slabs[c].at[pl.ds(s * sizes[c], sizes[c])], acts.at[s, pl.ds(starts[c], sizes[c])], act_sems.at[s, c]
            )
            for c in range(n)
            for s in range(2)
        ]
        copies = [pltpu.make_async_copy(w, held.at[i], sems.at[i]) for i, w in enumerate(weights)]
        for c in loads + copies:
            c.start()
        for c in loads:
            c.wait()
        for g in range(2):
            total = None
            for i in range(4):
                copies[4 * g + i].wait()
                here = core if i < 2 else 1 - core
                for t in range(2):
                    if g == 0:
                        slab, chip = t, (x if i % 2 == 0 else 1 - x)
                    else:
                        slab, chip = (y if i % 2 == 0 else 1 - y), t
                    at = pl.multiple_of((2 * chip + here) * share, 128)
                    a = acts[slab, :, pl.ds(at, share)]
                    w = held[4 * g + i, t * share : (t + 1) * share, :]
                    term = jnp.dot(a, w, preferred_element_type=jnp.float32)
                    total = term if total is None else total + term
            out[:, g * cols : (g + 1) * cols] = total.astype(jnp.bfloat16)


def finish_kernel(segments, whole, chained, plan, *refs):
    given = []
    at = 0
    for s in segments:
        n = len(s.accs) + len(s.parts)
        given.append(refs[at : at + n])
        at += n
    ssq_a, ssq_b, bk, bv, cosine, sine = refs[at : at + 6]
    refs = refs[at + 6 + (2 if chained else 0) :]
    k_out, v_out, acc_held, far_held, k_held, v_held, cos_held, sin_held, in_sems, rope_sems, out_sems = refs
    cols = k_held.shape[1]
    loads, spots = [], []
    for i, (s, arrays) in enumerate(zip(segments, given)):
        rows, here, count = s.rows, s.here, 2 * s.rows
        mine = [
            pltpu.make_async_copy(ref.at[pl.ds(row, count)], acc_held.at[t, pl.ds(here, count)], in_sems.at[i, t])
            for t, (row, ref) in enumerate(zip(s.accs, arrays))
        ]
        for p, ((row, col, wide), ref) in enumerate(zip(s.parts, arrays[len(s.accs) :])):
            mine.append(
                pltpu.make_async_copy(
                    ref.at[pl.ds(row, count)],
                    far_held.at[pl.ds(here, count), pl.ds(col, wide)],
                    in_sems.at[i, 2 + p],
                )
            )
        spots.append([pl.multiple_of(plan[s.first + j, 2] * BLOCK + s.low, 16) for j in range(2)])
        for j in range(2):
            for t, (src, dst) in enumerate(((cosine, cos_held), (sine, sin_held))):
                mine.append(
                    pltpu.make_async_copy(
                        src.at[pl.ds(spots[i][j], rows)], dst.at[pl.ds(here + j * rows, rows)], rope_sems.at[i, j, t]
                    )
                )
        for c in mine:
            c.start()
        loads.append(mine)
    stores = []
    for i, s in enumerate(segments):
        rows = s.rows
        for c in loads[i]:
            c.wait()
        for j in range(2):
            row = s.ssq + j
            sums = jnp.broadcast_to(ssq_a[row : row + 1, :] + ssq_b[row : row + 1, :], (8, BLOCK))
            scale = lax.rsqrt(sums.T[:rows, :1] * (1.0 / whole) + EPS)
            span = slice(s.here + j * rows, s.here + (j + 1) * rows)
            cos_rows, sin_rows = cos_held[span, :], sin_held[span, :]
            for h in range(cols // HD):
                lanes = slice(h * HD, (h + 1) * HD)
                k = acc_held[0, span, lanes]
                if len(s.accs) > 1:
                    k += acc_held[1, span, lanes]
                if s.parts:
                    k += far_held[span, lanes].astype(jnp.float32)
                k = k * scale + bk[:, lanes]
                k_held[span, lanes] = (k * cos_rows + pltpu.roll(k, HD // 2, 1) * sin_rows).astype(jnp.bfloat16)
                lanes_v = slice(cols + h * HD, cols + (h + 1) * HD)
                v = acc_held[0, span, lanes_v]
                if len(s.accs) > 1:
                    v += acc_held[1, span, lanes_v]
                if s.parts:
                    v += far_held[span, lanes_v].astype(jnp.float32)
                v_held[span, lanes] = (v * scale + bv[:, lanes]).astype(jnp.bfloat16)
            for t, (held, out) in enumerate(((k_held, k_out), (v_held, v_out))):
                stores.append(
                    pltpu.make_async_copy(
                        held.at[pl.ds(s.here + j * rows, rows)],
                        out.at[pl.ds(spots[i][j], rows)],
                        out_sems.at[i, j, t],
                    )
                )
                stores[-1].start()
    for c in stores:
        c.wait()


Segment = collections.namedtuple(
    "Segment", ("low", "rows", "first", "accs", "here", "ssq", "parts")
)


def grouped(cached_rows, counts, dest_table, positions, norm_gain, key_weight, value_weight, key_bias, value_bias):
    stores = lax.axis_size("store")
    z, y = lax.axis_index("tensor"), lax.axis_index("groups")
    tokens = positions.shape[0]
    per_row = tokens // BLOCK
    most = dest_table.shape[1] // stores
    cached = cached_rows[0]
    width = cached.shape[1]
    whole, cols = key_weight.shape
    share = whole // 16
    dma = pltpu.SemaphoreType.DMA
    bf16 = functools.partial(jax.ShapeDtypeStruct, dtype=jnp.bfloat16)
    f32 = functools.partial(jax.ShapeDtypeStruct, dtype=jnp.float32)
    swap = {m: ("store", [(s, s ^ m) for s in range(stores)]) for m in range(1, stores)}
    pair = ("tensor", [(0, 1), (1, 0), (2, 3), (3, 2)])
    middle = ("tensor", [(1, 2), (2, 1)])
    inward = ("tensor", [(0, 1), (3, 2)])
    outward = ("tensor", [(1, 0), (2, 3)])
    across = ("groups", [(0, 1), (1, 0)])
    ends = ("tensor", [(0, 3), (1, 2), (2, 1), (3, 0)])

    inner = (z == 1) | (z == 2)
    other = [jnp.where(inner, 3 - z, z ^ 2), jnp.where(inner, (3 - z) ^ 1, 3 - z)]
    chip, core = lax.axis_index("store") // 2, lax.rem(lax.axis_index("store"), 2)
    info = jnp.stack([z, z ^ 1, *other, inner.astype(jnp.int32), y, chip, core]).astype(jnp.int32)
    gain = norm_gain[None, :]

    call = Chain()
    came, own, ssq, ex, mr, fw, accs, far = {}, {}, {}, {}, {}, {}, {}, {}
    done = []

    def move(label, array, way):
        with jax.named_scope(label):
            return lax.ppermute(array, *way)

    def send(*parts):
        shapes = [bf16((sum(s[2] for _, _, s in p), width)) for p in parts]
        return call(
            functools.partial(send_kernel, parts, per_row),
            "send",
            (dest_table, cached),
            [SMEM, HBM],
            shapes,
            [VMEM] * len(shapes),
            [dma((sum(len(p) for p in parts),))],
        )

    def prep(c, cost=COST):
        k, low, rows = CHUNKS[c]
        pieces, arrays = [], []
        for r in range(k + 1):
            pieces.append((r, 1, 0, BLOCK, 0 if r == 0 else (most + r - 2) * BLOCK))
            arrays.append(beside[min(r, 1)])
        for i, (r, p_low, p_rows) in enumerate(STEPS):
            if r <= k and p_low < low + rows and low < p_low + p_rows:
                for m in (2, 3):
                    array, at = came[i][m]
                    pieces.append((r, m, p_low, p_rows, at))
                    arrays.append(array)
        own[c], ssq[c] = call(
            functools.partial(prep_kernel, low, rows, 2 * k, stores, pieces),
            "prep",
            (plan, cached, *arrays, gain),
            [SMEM, HBM] + [HBM] * len(pieces) + [VMEM],
            [bf16((2 * rows, width)), f32((2, BLOCK))],
            [VMEM, VMEM],
            [pltpu.VMEM((2, rows, width), jnp.bfloat16), dma((2,))],
            cost=cost,
        )

    def pass_own(c):
        ex[c] = move("ex%d" % c, own[c], pair)

    def relay(c):
        rows = 2 * CHUNKS[c][2]
        (both,) = call(
            relay_kernel, "relay", (own[c], ex[c]), [HBM] * 2, [bf16((2 * rows, width))], [VMEM], [dma((2,))]
        )
        mr[c] = move("mr%d" % c, both, middle)

    def pin(*arrays, cost=COST):
        return call.pin("pin", arrays, cost)

    def hand(c):
        fw[c] = move("fw%d" % c, mr[c], outward)

    def sums(step, *arrays):
        (out,) = call(
            functools.partial(sums_kernel, step), "sums", arrays, [VMEM] * len(arrays), [f32((16, BLOCK))], [VMEM]
        )
        return out

    handed = (0, 1, 2)

    def near(taken, first, last):
        sizes = [2 * CHUNKS[c][2] for c in taken]
        total = sum(sizes)
        rows_handed = sum(size for c, size in zip(taken, sizes) if last == 4 and c in handed)
        kinds = ((own, ex) if first == 0 else ()) + ((mr,) if last == 4 else ())
        groups = [[k[c] for k in kinds] + ([fw[c]] if last == 4 and c in handed else []) for c in taken]
        slabs = [array for group in groups for array in group]
        counts_in = [len(group) for group in groups]

        def weights(i, info):
            slab = first + i // 2
            skip = (slab >= 2) & (info[4] == 0) & (rows_handed == 0)
            return (jnp.where(skip, info[1] * 2 + 1, info[slab] * 2 + lax.rem(i, 2)), 0)

        (acc,) = call(
            functools.partial(near_kernel, sizes, first, rows_handed, counts_in),
            "near",
            (info, *slabs, key_weight, value_weight),
            [HBM] * len(slabs) + [pl.BlockSpec((width // 2, cols), weights)] * 2,
            [f32((total, 2 * cols))],
            [pl.BlockSpec((total, 2 * cols), lambda i, info: (0, 0))],
            [pltpu.VMEM((last - first, total, width), jnp.bfloat16), dma((last - first, len(sizes)))],
            grid=(2 * (last - first),),
        )
        for i, c in enumerate(taken):
            accs.setdefault(c, []).append((acc, sum(sizes[:i])))

    def reach(*taken):
        sizes = [2 * CHUNKS[c][2] for c in taken]
        total = sum(sizes)
        (out,) = call(
            functools.partial(far_kernel, sizes),
            "far",
            (info, *(mr[c] for c in taken), *reached),
            [SMEM] + [HBM] * (len(taken) + len(reached)),
            [bf16((total, 2 * cols))],
            [VMEM],
            [
                pltpu.VMEM((2, total, width), jnp.bfloat16),
                pltpu.VMEM((8, *reached[0].shape), jnp.bfloat16),
                dma((2, len(sizes))),
                dma((8,)),
            ],
        )
        out = move("far%d" % taken[0], out, outward)
        for i, c in enumerate(taken):
            far.setdefault(c, []).append((out, (sum(sizes[:i]), 0, 2 * cols)))

    def finish(*taken):
        segments, arrays, here = [], [], 0
        for c in taken:
            k, low, rows = CHUNKS[c]
            arrays += [a for a, _ in accs[c]] + [a for a, _ in far.get(c, [])]
            segments.append(
                Segment(low, rows, 2 * k, [r for _, r in accs[c]], here, 2 * c, [p for _, p in far.get(c, [])])
            )
            here += 2 * rows
        most_accs = max(len(s.accs) for s in segments)
        args = [plan, *arrays, *total_squares, key_bias[None, :], value_bias[None, :], cosine, sine, *done]
        done[:] = call(
            functools.partial(finish_kernel, segments, whole, bool(done)),
            "finish",
            tuple(args),
            [SMEM] + [HBM] * len(arrays) + [VMEM] * 4 + [HBM] * (2 + len(done)),
            [bf16((tokens, cols))] * 2,
            [HBM] * 2,
            [
                pltpu.VMEM((most_accs, here, 2 * cols), jnp.float32),
                pltpu.VMEM((here, 2 * cols), jnp.bfloat16),
                pltpu.VMEM((here, cols), jnp.bfloat16),
                pltpu.VMEM((here, cols), jnp.bfloat16),
                pltpu.VMEM((here, HD), jnp.float32),
                pltpu.VMEM((here, HD), jnp.float32),
                dma((len(segments), 4)),
                dma((len(segments), 2, 2)),
                dma((len(segments), 2, 2)),
            ],
            aliases={len(args) - 2: 0, len(args) - 1: 1} if done else None,
        )

    def both_ways(i):
        return [[(0, m, STEPS[i])] for m in (2, 3)]

    def exchange(i, sent):
        came[i] = {m: (move("a%d" % i, array, swap[m]), 0) for m, array in zip((2, 3), sent)}

    tables = [move("table", dest_table, swap[m]) for m in range(1, stores)]
    *s0, close = send(*both_ways(0), [(0, 1, (0, 0, BLOCK))])
    exchange(0, s0)
    beside = [move("b0", close, swap[1])]
    (plan,) = call(
        functools.partial(plan_kernel, stores, per_row),
        "plan",
        (dest_table, *tables),
        [SMEM] * stores,
        [jax.ShapeDtypeStruct((per_row, 4), jnp.int32)],
        [SMEM],
    )
    def join(axis, here, hopped, *before):
        return call(
            functools.partial(join_kernel, axis),
            "join",
            (info, here, hopped, *before),
            [SMEM] + [HBM] * (2 + axis),
            [bf16((2 * share, cols)), bf16((4 * share, cols))][: 1 + axis],
            [VMEM] * (1 + axis),
            [dma((3, 2))],
        )

    onward = [((k - 1) * BLOCK, 3, (k, 0, BLOCK)) for k in range(1, most)]
    onward += [((most + k - 2) * BLOCK, 1, (k, 0, BLOCK)) for k in range(1, most)]
    *s1, passed = send(*both_ways(1), onward)
    exchange(1, s1)
    passed = move("pass", passed, swap[1])
    beside.append(passed)
    prep(0, FAR)
    pass_own(0)
    packs = call(
        functools.partial(pack_kernel, per_row),
        "pack",
        (dest_table, cached, passed),
        [SMEM, HBM, HBM],
        [bf16((2 * BLOCK, width))] * 3,
        [VMEM] * 3,
        [dma((3, 2))],
    )

    cuts = call(
        cut_kernel, "cut", (key_weight, value_weight), [HBM] * 2, [bf16((share, cols))] * 2, [VMEM] * 2, [dma((2,))]
    )

    def hop(k, pack):
        hopped = move("h%d" % k, pack, swap[2])
        came[k + 1] = {2: (hopped, 0), 3: (hopped, BLOCK)}

    prep(1)
    pass_own(1)
    pack, lent_k = pin(packs[0], cuts[0])
    hop(1, pack)
    lent_k = move("ink", lent_k, inward)
    relay(0)
    relay(1)
    prep(2)
    pass_own(2)
    (pack,) = pin(packs[1])
    hop(2, pack)
    (positions,) = pin(positions)
    cosine, sine = pin(*rope_tables(positions))
    mr[0], lent_k, lent_v = pin(mr[0], lent_k, cuts[1])
    hand(0)
    lent_v = move("inv", lent_v, inward)
    near((0, 1), 0, 2)
    relay(2)
    prep(3)
    pass_own(3)
    mr[1], pack = pin(mr[1], packs[2])
    hop(3, pack)
    fw[0], lent_v, lent_k, mr[1] = pin(fw[0], lent_v, lent_k, mr[1])
    hand(1)
    came_k = move("wk1", lent_k, across)
    (lent_v,) = pin(lent_v)
    came_v = move("wv1", lent_v, swap[2])
    near((2,), 0, 2)
    relay(3)
    (mr[2],) = pin(mr[2])
    prep(4)
    squares = sums(0, *(ssq[c] for c in range(len(CHUNKS))))
    paired = move("half", squares, pair)
    fw[1], own[4] = pin(fw[1], own[4])
    pass_own(4)
    (joined_k,) = join(0, lent_k, came_k)
    came_k = move("wk2", joined_k, swap[2])
    joined_v, joined = join(1, lent_v, came_v, joined_k)
    came_v = move("wv2", joined_v, across)
    mr[2], paired = pin(mr[2], paired)
    hand(2)
    near((3, 4), 0, 2)
    (mr[3],) = pin(mr[3])
    squares = sums(1, squares, paired)
    rest = move("rest", squares, ends)
    relay(4)
    near((0, 1), 2, 4)
    came_k, came_v, joined = pin(came_k, came_v, joined)
    beside_w = [move("core", w, swap[1]) for w in (joined, came_k, came_v)]
    total_squares = (squares, rest)
    finish(0, 1)
    (fw[2],) = pin(fw[2], cost=FAR)
    reached = (joined_k, joined_v, came_k, came_v, *beside_w)
    reach(3)
    reach(4)
    near((2, 3, 4), 2, 4)
    finish(2, 3)
    finish(4)
    return tuple(done)


def slot_ranks(dest_table, counts, per_row):
    slot_ids = jnp.arange(dest_table.shape[1], dtype=jnp.int32)
    is_valid = slot_ids[None, :] < counts[:, None]
    row_ids = jnp.where(is_valid, dest_table // per_row, -1)
    earlier = (
        (row_ids[:, :, None] == row_ids[:, None, :])
        & (slot_ids[None, None, :] < slot_ids[None, :, None])
        & is_valid[:, None, :]
    )
    return is_valid, row_ids, jnp.sum(earlier.astype(jnp.int32), axis=2)


def rotate_keys(key_raw, positions):
    rows, cols = key_raw.shape
    cosine, sine = rope_tables(positions)
    heads = key_raw.reshape(rows, cols // HD, HD)
    turned = heads * cosine[:, None, :] + jnp.roll(heads, HD // 2, axis=2) * sine[:, None, :]
    return turned.reshape(rows, cols)


def gathered(cached_rows, counts, dest_table, positions, norm_gain, key_weight, value_weight, key_bias, value_bias):
    stores = lax.axis_size("store")
    own_row = lax.axis_index("store")
    capacity = dest_table.shape[1]
    per_pair = capacity // stores
    per_row = positions.shape[0] // BLOCK
    width = cached_rows.shape[2]
    flat_slots = cached_rows.reshape(capacity, BLOCK * width)
    all_counts = lax.all_gather(counts, "store", axis=0, tiled=True)
    all_table = lax.all_gather(dest_table, "store", axis=0, tiled=True)
    is_valid, _, row_rank = slot_ranks(all_table, all_counts, per_row)
    target = own_row * per_row + jnp.arange(per_row, dtype=jnp.int32)
    own_valid, own_rows, own_rank = slot_ranks(dest_table, counts, per_row)
    pick = (
        own_valid[0][None, None, :]
        & (own_rows[0][None, None, :] == jnp.arange(stores, dtype=jnp.int32)[:, None, None])
        & (own_rank[0][None, None, :] == jnp.arange(per_pair, dtype=jnp.int32)[None, :, None])
    ).astype(jnp.bfloat16)
    outgoing = jnp.einsum("rkj,jf->rkf", pick, flat_slots, preferred_element_type=jnp.float32)
    arrived = lax.all_to_all(outgoing.astype(jnp.bfloat16), "store", split_axis=0, concat_axis=0, tiled=True)
    placing = (
        is_valid[None, :, :, None]
        & (all_table[None, :, :, None] == target[:, None, None, None])
        & (row_rank[None, :, :, None] == jnp.arange(per_pair, dtype=jnp.int32)[None, None, None, :])
    )
    placing = jnp.sum(placing.astype(jnp.int32), axis=2).astype(jnp.bfloat16)
    local = jnp.einsum("bsk,skf->bf", placing, arrived, preferred_element_type=jnp.float32)
    local = local.astype(jnp.bfloat16).reshape(per_row * BLOCK, width)
    rows = lax.all_gather(local, "tensor", axis=1, tiled=True).astype(jnp.float32)
    scale = lax.rsqrt(jnp.mean(rows * rows, axis=1) + EPS)
    normed = (rows * scale[:, None] * norm_gain[None, :]).astype(jnp.bfloat16)
    keys = jnp.dot(normed, key_weight, preferred_element_type=jnp.float32) + key_bias[None, :]
    values = jnp.dot(normed, value_weight, preferred_element_type=jnp.float32) + value_bias[None, :]
    return rotate_keys(keys, positions).astype(jnp.bfloat16), values.astype(jnp.bfloat16)


def solution(mesh):
    in_specs = (
        P(("groups", "store"), None, "tensor"),
        P(("groups", "store")),
        P(("groups", "store"), None),
        P(("groups", "store")),
        P(),
        P(None, "tensor"),
        P(None, "tensor"),
        P("tensor"),
        P("tensor"),
    )
    out_specs = (P(("groups", "store"), "tensor"), P(("groups", "store"), "tensor"))
    small = tuple(mesh.shape[axis] for axis in ("groups", "store", "tensor")) == (2, 4, 4)
    body = grouped if small else gathered
    return jax.shard_map(body, mesh=mesh, in_specs=in_specs, out_specs=out_specs, check_vma=False)
```

```python
import collections
import functools

import jax
import jax.numpy as jnp
from jax import lax
from jax.experimental import pallas as pl
from jax.experimental.pallas import tpu as pltpu
from jax.sharding import PartitionSpec as P

HD = 128
BLOCK = 128
ROPE_BASE = 1000000.0
EPS = 1e-06
MIB = 1 << 20
VMEM_LIMIT = 63 * MIB
COST = 4 * 10**9
FAR = 10**11
HBM = pl.BlockSpec(memory_space=pltpu.HBM)
SMEM = pl.BlockSpec(memory_space=pltpu.SMEM)
VMEM = pl.BlockSpec(memory_space=pltpu.VMEM)
TOKEN = jax.ShapeDtypeStruct((8, 128), jnp.int32)

STEPS = ((0, 0, 64), (0, 64, 64), (1, 0, 128), (2, 0, 128), (3, 0, 128))
CHUNKS = ((0, 0, 64), (0, 64, 64), (1, 0, 128), (2, 0, 128), (3, 0, 128))


def rope_tables(positions):
    half = HD // 2
    inverse = 1.0 / ROPE_BASE ** (jnp.arange(half, dtype=jnp.float32) * 2.0 / HD)
    angles = positions.astype(jnp.float32)[:, None] * inverse[None, :]
    cosine, sine = jnp.cos(angles), jnp.sin(angles)
    return (
        jnp.concatenate([cosine, cosine], axis=1),
        jnp.concatenate([-sine, sine], axis=1),
    )


class Chain:
    def __init__(self):
        self.token = None

    def __call__(self, kernel, name, args, specs, outs, out_specs, scratch=(), grid=None, aliases=None, cost=COST):
        first = self.token is None
        prefetch = 0 if grid is None else 1
        taken, given = len(args), len(outs)

        def body(*refs):
            ins = refs[:taken]
            after = taken + (0 if first else 1)
            kernel(*ins, *refs[after : after + given], *refs[after + given + 1 :])

        tokens = () if first else (self.token,)
        in_specs = list(specs) + [HBM] * len(tokens)
        out_specs = list(out_specs) + [HBM]
        if grid is None:
            where = dict(in_specs=in_specs, out_specs=out_specs, scratch_shapes=list(scratch))
        else:
            where = dict(
                grid_spec=pltpu.PrefetchScalarGridSpec(
                    num_scalar_prefetch=prefetch,
                    grid=grid,
                    in_specs=in_specs,
                    out_specs=out_specs,
                    scratch_shapes=list(scratch),
                )
            )
        result = pl.pallas_call(
            body,
            out_shape=tuple(outs) + (TOKEN,),
            input_output_aliases=aliases or {},
            compiler_params=pltpu.CompilerParams(vmem_limit_bytes=VMEM_LIMIT),
            cost_estimate=pl.CostEstimate(flops=cost, bytes_accessed=1, transcendentals=0),
            name=name,
            **where,
        )(*args, *tokens)
        self.token = result[-1]
        return result[:-1]

    def pin(self, name, arrays, cost=COST):
        outs = [jax.ShapeDtypeStruct(a.shape, a.dtype) for a in arrays]
        n = len(arrays)
        return self(
            lambda *refs: None, name, arrays, [HBM] * n, outs, [HBM] * n, aliases={i: i for i in range(n)}, cost=cost
        )


def in_row(table, low, per_row):
    start, count = jnp.int32(0), jnp.int32(0)
    for s in range(table.shape[1]):
        block = table[0, s]
        start += ((block >= 0) & (block < low)).astype(jnp.int32)
        count += ((block >= low) & (block < low + per_row)).astype(jnp.int32)
    return start, count


def plan_kernel(stores, per_row, *refs):
    tables, plan = refs[:-1], refs[-1]
    low = lax.axis_index("store") * per_row
    spans = [in_row(t, low, per_row) for t in tables]
    n = jnp.int32(0)
    for i in range(per_row):
        for f in range(3):
            plan[i, f] = jnp.int32(0)
    for r in range(tables[0].shape[1] // stores):
        for m in range(stores):
            start, count = spans[m]
            valid = r < count

            @pl.when(valid)
            def _():
                plan[n, 0] = jnp.int32(r * stores + m)
                plan[n, 1] = start + r
                plan[n, 2] = tables[m][0, start + r] - low

            n += valid.astype(jnp.int32)


def send_kernel(steps, per_row, table, cached, *refs):
    outs, sems = refs[:-1], refs[-1]
    own_row = lax.axis_index("store")
    last = table.shape[1] - 1
    starts = {m: in_row(table, (own_row ^ m) * per_row, per_row)[0] for m in {m for s in steps for _, m, _ in s}}
    copies = []
    for out, parts in zip(outs, steps):
        for at, m, (k, low, rows) in parts:
            src = pl.multiple_of(jnp.minimum(starts[m] + k, last) * BLOCK + low, 16)
            copies.append(
                pltpu.make_async_copy(cached.at[pl.ds(src, rows)], out.at[pl.ds(at, rows)], sems.at[len(copies)])
            )
            copies[-1].start()
    for c in copies:
        c.wait()


def pack_kernel(per_row, table, cached, passed, *refs):
    outs, sems = refs[:-1], refs[-1]
    start, _ = in_row(table, (lax.axis_index("store") ^ 2) * per_row, per_row)
    copies = []
    for i, out in enumerate(outs):
        src = pl.multiple_of(jnp.minimum(start + i + 1, table.shape[1] - 1) * BLOCK, 16)
        copies.append(pltpu.make_async_copy(cached.at[pl.ds(src, BLOCK)], out.at[pl.ds(0, BLOCK)], sems.at[i, 0]))
        here = passed.at[pl.ds(i * BLOCK, BLOCK)]
        copies.append(pltpu.make_async_copy(here, out.at[pl.ds(BLOCK, BLOCK)], sems.at[i, 1]))
    for c in copies:
        c.start()
    for c in copies:
        c.wait()


def cut_kernel(key_weight, value_weight, *refs):
    outs, sems = refs[:-1], refs[-1]
    z, y, own_row = lax.axis_index("tensor"), lax.axis_index("groups"), lax.axis_index("store")
    share = outs[0].shape[0]
    slab = jnp.where(z == 0, 2 + y, 1 - y)
    at = pl.multiple_of((slab * 4 + own_row) * share, 128)
    copies = [
        pltpu.make_async_copy(weight.at[pl.ds(at, share)], out, sems.at[g])
        for g, (weight, out) in enumerate(zip((key_weight, value_weight), outs))
    ]
    for c in copies:
        c.start()
    for c in copies:
        c.wait()


def join_kernel(axis, info, here, came, *refs):
    before, outs, sems = refs[:axis], refs[axis:-1], refs[-1]
    share = here.shape[0]
    place = info[5 + axis]
    copies = []
    for t, src in enumerate((here, came)):
        at = pl.multiple_of((place if t == 0 else 1 - place) * share, 128)
        copies.append(pltpu.make_async_copy(src, outs[0].at[pl.ds(at, share)], sems.at[0, t]))
        if axis == 1:
            copies.append(pltpu.make_async_copy(src, outs[1].at[pl.ds(at + 2 * share, share)], sems.at[1, t]))
    if axis == 1:
        copies.append(pltpu.make_async_copy(before[0], outs[1].at[pl.ds(0, 2 * share)], sems.at[2, 0]))
    for c in copies:
        c.start()
    for c in copies:
        c.wait()


def prep_kernel(low, rows, first, stores, pieces, plan, cached, *refs):
    arrived = refs[: len(pieces)]
    gain, y_out, ssq_out, held, sems = refs[len(pieces) :]
    width = held.shape[2]
    z = lax.axis_index("tensor")
    for j in range(2):
        code = plan[first + j, 0]

        @pl.when(lax.rem(code, stores) == 0)
        def _():
            start = pl.multiple_of(plan[first + j, 1] * BLOCK + low, 16)
            pltpu.make_async_copy(cached.at[pl.ds(start, rows)], held.at[j], sems.at[j]).start()

        for (r, m, p_low, p_rows, at), ref in zip(pieces, arrived):
            a, b = max(low, p_low), min(low + rows, p_low + p_rows)

            @pl.when(code == r * stores + m)
            def _():
                pltpu.make_async_copy(
                    ref.at[pl.ds(at + a - p_low, b - a)], held.at[j, pl.ds(a - low, b - a)], sems.at[j]
                ).start()

    for j in range(2):
        pltpu.make_async_copy(cached.at[pl.ds(0, rows)], held.at[j], sems.at[j]).wait()
        sums = jnp.zeros((rows, 128), jnp.float32)
        for c in range(0, width, 128):
            x = held[j, :, c : c + 128].astype(jnp.float32)
            here = gain[:, pl.ds(pl.multiple_of(z * width + c, 128), 128)]
            y_out[j * rows : (j + 1) * rows, c : c + 128] = (x * here).astype(jnp.bfloat16)
            sums += x * x
        ssq_out[j : j + 1, :rows] = jnp.sum(sums.T, axis=0, keepdims=True)


def copy_kernel(given, out):
    out[...] = given[...]


def sums_kernel(step, *refs):
    out = refs[-1]
    if step == 0:
        out[...] = jnp.zeros_like(out)
        for i, ref in enumerate(refs[:-1]):
            out[2 * i : 2 * i + 2, :] = ref[...]
    else:
        out[...] = refs[0][...] + refs[1][...]


def relay_kernel(own, ex, out, sems):
    rows = own.shape[0]
    copies = [
        pltpu.make_async_copy(src, out.at[pl.ds(i * rows, rows)], sems.at[i]) for i, src in enumerate((own, ex))
    ]
    for c in copies:
        c.start()
    for c in copies:
        c.wait()


def near_kernel(sizes, first, lead, counts, info, *refs):
    n = len(sizes)
    wk, wv, acc, acts, sems = refs[-5:]
    arrays = [refs[sum(counts[:c]) : sum(counts[: c + 1])] for c in range(n)]
    slabs = acts.shape[0]
    i = pl.program_id(0)
    slab, half = first + i // 2, lax.rem(i, 2)
    inner = info[4] == 1
    starts = [sum(sizes[:c]) for c in range(n)]

    def copies(s, which, skip=0, rows=sum(sizes)):
        return [
            pltpu.make_async_copy(
                arrays[c][which].at[pl.ds(skip * sizes[c], sizes[c])],
                acts.at[s - first, pl.ds(starts[c], sizes[c])],
                sems.at[s - first, c],
            )
            for c in range(n)
            if starts[c] < rows
        ]

    def held(s, fetch):
        if s < 2:
            fetch(copies(s, s))
        else:

            @pl.when(inner)
            def _():
                fetch(copies(s, 2 - first, s - 2))

            if lead:

                @pl.when(jnp.logical_not(inner))
                def _():
                    fetch(copies(s, 3 - first, s - 2, lead))

    def start(made):
        for c in made:
            c.start()

    def wait(made):
        for c in made:
            c.wait()

    @pl.when(i == 0)
    def _():
        for s in range(first, first + slabs):
            held(s, start)

    for s in range(first, first + slabs):

        @pl.when((half == 0) & (slab == s))
        def _():
            held(s, wait)

    part, cols = wk.shape

    @pl.when(i == 0)
    def _():
        acc[...] = jnp.zeros_like(acc)

    def add(rows):
        a = acts[slab - first, :rows, pl.ds(pl.multiple_of(half * part, part), part)]
        acc[:rows, :cols] += jnp.dot(a, wk[...], preferred_element_type=jnp.float32)
        acc[:rows, cols:] += jnp.dot(a, wv[...], preferred_element_type=jnp.float32)

    whole_rows = (slab < 2) | inner if lead < sum(sizes) else i >= 0

    @pl.when(whole_rows)
    def _():
        add(sum(sizes))

    if 0 < lead < sum(sizes):

        @pl.when(jnp.logical_not(whole_rows))
        def _():
            add(lead)


def far_kernel(sizes, info, *refs):
    n = len(sizes)
    slabs = refs[:n]
    joined_k, joined_v, came_k, came_v, joined, beside_k, beside_v = refs[n : n + 7]
    out, acts, held, act_sems, sems = refs[n + 7 :]
    starts = [sum(sizes[:c]) for c in range(n)]
    rows, cols = held.shape[1:]
    share = rows // 2
    weights = (joined_k, came_k, joined.at[pl.ds(0, rows)], beside_k)
    weights += (joined_v, came_v, joined.at[pl.ds(rows, rows)], beside_v)
    y, x, core = info[5], info[6], info[7]

    @pl.when(info[4] == 1)
    def _():
        loads = []
        for g in range(2):
            for i in range(4):
                here = core if i < 2 else 1 - core
                for t in range(2):
                    if g == 0:
                        slab, chip = t, (x if i % 2 == 0 else 1 - x)
                    else:
                        slab, chip = (y if i % 2 == 0 else 1 - y), t
                    at = pl.multiple_of((2 * chip + here) * share, 128)
                    for c in range(n):
                        row = pl.multiple_of(slab * sizes[c], 16)
                        loads.append(
                            pltpu.make_async_copy(
                                slabs[c].at[pl.ds(row, sizes[c]), pl.ds(at, share)],
                                acts.at[4 * g + i, pl.ds(starts[c], sizes[c]), pl.ds(t * share, share)],
                                act_sems.at[4 * g + i, t, c],
                            )
                        )
        copies = [pltpu.make_async_copy(w, held.at[i], sems.at[i]) for i, w in enumerate(weights)]
        for i, c in enumerate(copies):
            for load in loads[2 * n * i : 2 * n * (i + 1)]:
                load.start()
            c.start()
        for g in range(2):
            total = None
            for i in range(4 * g, 4 * g + 4):
                for load in loads[2 * n * i : 2 * n * (i + 1)]:
                    load.wait()
                copies[i].wait()
                term = jnp.dot(acts[i], held[i], preferred_element_type=jnp.float32)
                total = term if total is None else total + term
            out[:, g * cols : (g + 1) * cols] = total.astype(jnp.bfloat16)


def finish_kernel(segments, whole, chained, plan, *refs):
    given = []
    at = 0
    for s in segments:
        n = len(s.accs) + len(s.parts)
        given.append(refs[at : at + n])
        at += n
    ssq_a, ssq_b, bk, bv, cosine, sine = refs[at : at + 6]
    refs = refs[at + 6 + (2 if chained else 0) :]
    k_out, v_out, acc_held, far_held, k_held, v_held, cos_held, sin_held, in_sems, rope_sems, out_sems = refs
    cols = k_held.shape[1]
    loads, spots = [], []
    for i, (s, arrays) in enumerate(zip(segments, given)):
        rows, here, count = s.rows, s.here, 2 * s.rows
        mine = [
            pltpu.make_async_copy(ref.at[pl.ds(row, count)], acc_held.at[t, pl.ds(here, count)], in_sems.at[i, t])
            for t, (row, ref) in enumerate(zip(s.accs, arrays))
        ]
        for p, ((row, col, wide), ref) in enumerate(zip(s.parts, arrays[len(s.accs) :])):
            mine.append(
                pltpu.make_async_copy(
                    ref.at[pl.ds(row, count)],
                    far_held.at[pl.ds(here, count), pl.ds(col, wide)],
                    in_sems.at[i, 2 + p],
                )
            )
        spots.append([pl.multiple_of(plan[s.first + j, 2] * BLOCK + s.low, 16) for j in range(2)])
        for j in range(2):
            for t, (src, dst) in enumerate(((cosine, cos_held), (sine, sin_held))):
                mine.append(
                    pltpu.make_async_copy(
                        src.at[pl.ds(spots[i][j], rows)], dst.at[pl.ds(here + j * rows, rows)], rope_sems.at[i, j, t]
                    )
                )
        for c in mine:
            c.start()
        loads.append(mine)
    stores = []
    for i, s in enumerate(segments):
        rows = s.rows
        for c in loads[i]:
            c.wait()
        for j in range(2):
            row = s.ssq + j
            sums = jnp.broadcast_to(ssq_a[row : row + 1, :] + ssq_b[row : row + 1, :], (8, BLOCK))
            scale = lax.rsqrt(sums.T[:rows, :1] * (1.0 / whole) + EPS)
            span = slice(s.here + j * rows, s.here + (j + 1) * rows)
            cos_rows, sin_rows = cos_held[span, :], sin_held[span, :]
            for h in range(cols // HD):
                lanes = slice(h * HD, (h + 1) * HD)
                k = acc_held[0, span, lanes]
                if len(s.accs) > 1:
                    k += acc_held[1, span, lanes]
                if s.parts:
                    k += far_held[span, lanes].astype(jnp.float32)
                k = k * scale + bk[:, lanes]
                k_held[span, lanes] = (k * cos_rows + pltpu.roll(k, HD // 2, 1) * sin_rows).astype(jnp.bfloat16)
                lanes_v = slice(cols + h * HD, cols + (h + 1) * HD)
                v = acc_held[0, span, lanes_v]
                if len(s.accs) > 1:
                    v += acc_held[1, span, lanes_v]
                if s.parts:
                    v += far_held[span, lanes_v].astype(jnp.float32)
                v_held[span, lanes] = (v * scale + bv[:, lanes]).astype(jnp.bfloat16)
            for t, (held, out) in enumerate(((k_held, k_out), (v_held, v_out))):
                stores.append(
                    pltpu.make_async_copy(
                        held.at[pl.ds(s.here + j * rows, rows)],
                        out.at[pl.ds(spots[i][j], rows)],
                        out_sems.at[i, j, t],
                    )
                )
                stores[-1].start()
    for c in stores:
        c.wait()


Segment = collections.namedtuple(
    "Segment", ("low", "rows", "first", "accs", "here", "ssq", "parts")
)


def grouped(cached_rows, counts, dest_table, positions, norm_gain, key_weight, value_weight, key_bias, value_bias):
    stores = lax.axis_size("store")
    z, y = lax.axis_index("tensor"), lax.axis_index("groups")
    tokens = positions.shape[0]
    per_row = tokens // BLOCK
    most = dest_table.shape[1] // stores
    cached = cached_rows[0]
    width = cached.shape[1]
    whole, cols = key_weight.shape
    share = whole // 16
    dma = pltpu.SemaphoreType.DMA
    bf16 = functools.partial(jax.ShapeDtypeStruct, dtype=jnp.bfloat16)
    f32 = functools.partial(jax.ShapeDtypeStruct, dtype=jnp.float32)
    swap = {m: ("store", [(s, s ^ m) for s in range(stores)]) for m in range(1, stores)}
    pair = ("tensor", [(0, 1), (1, 0), (2, 3), (3, 2)])
    middle = ("tensor", [(1, 2), (2, 1)])
    inward = ("tensor", [(0, 1), (3, 2)])
    outward = ("tensor", [(1, 0), (2, 3)])
    across = ("groups", [(0, 1), (1, 0)])
    ends = ("tensor", [(0, 3), (1, 2), (2, 1), (3, 0)])

    inner = (z == 1) | (z == 2)
    other = [jnp.where(inner, 3 - z, z ^ 2), jnp.where(inner, (3 - z) ^ 1, 3 - z)]
    chip, core = lax.axis_index("store") // 2, lax.rem(lax.axis_index("store"), 2)
    info = jnp.stack([z, z ^ 1, *other, inner.astype(jnp.int32), y, chip, core]).astype(jnp.int32)
    gain = norm_gain[None, :]

    call = Chain()
    came, own, ssq, ex, mr, fw, accs, far = {}, {}, {}, {}, {}, {}, {}, {}
    done = []

    def move(label, array, way):
        with jax.named_scope(label):
            return lax.ppermute(array, *way)

    def send(*parts):
        shapes = [bf16((sum(s[2] for _, _, s in p), width)) for p in parts]
        return call(
            functools.partial(send_kernel, parts, per_row),
            "send",
            (dest_table, cached),
            [SMEM, HBM],
            shapes,
            [VMEM] * len(shapes),
            [dma((sum(len(p) for p in parts),))],
        )

    def prep(c, cost=COST):
        k, low, rows = CHUNKS[c]
        pieces, arrays = [], []
        for r in range(k + 1):
            pieces.append((r, 1, 0, BLOCK, 0 if r == 0 else (most + r - 2) * BLOCK))
            arrays.append(beside[min(r, 1)])
        for i, (r, p_low, p_rows) in enumerate(STEPS):
            if r <= k and p_low < low + rows and low < p_low + p_rows:
                for m in (2, 3):
                    array, at = came[i][m]
                    pieces.append((r, m, p_low, p_rows, at))
                    arrays.append(array)
        own[c], ssq[c] = call(
            functools.partial(prep_kernel, low, rows, 2 * k, stores, pieces),
            "prep",
            (plan, cached, *arrays, gain),
            [SMEM, HBM] + [HBM] * len(pieces) + [VMEM],
            [bf16((2 * rows, width)), f32((2, BLOCK))],
            [VMEM, VMEM],
            [pltpu.VMEM((2, rows, width), jnp.bfloat16), dma((2,))],
            cost=cost,
        )

    def pass_own(c):
        ex[c] = move("ex%d" % c, own[c], pair)

    def relay(c):
        rows = 2 * CHUNKS[c][2]
        (both,) = call(
            relay_kernel, "relay", (own[c], ex[c]), [HBM] * 2, [bf16((2 * rows, width))], [VMEM], [dma((2,))]
        )
        mr[c] = move("mr%d" % c, both, middle)

    def pin(*arrays, cost=COST):
        return call.pin("pin", arrays, cost)

    def hand(c):
        fw[c] = move("fw%d" % c, mr[c], outward)

    def sums(step, *arrays):
        (out,) = call(
            functools.partial(sums_kernel, step), "sums", arrays, [VMEM] * len(arrays), [f32((16, BLOCK))], [VMEM]
        )
        return out

    handed = (0, 1, 2)

    def near(taken, first, last):
        sizes = [2 * CHUNKS[c][2] for c in taken]
        total = sum(sizes)
        rows_handed = sum(size for c, size in zip(taken, sizes) if last == 4 and c in handed)
        kinds = ((own, ex) if first == 0 else ()) + ((mr,) if last == 4 else ())
        groups = [[k[c] for k in kinds] + ([fw[c]] if last == 4 and c in handed else []) for c in taken]
        slabs = [array for group in groups for array in group]
        counts_in = [len(group) for group in groups]

        def weights(i, info):
            slab = first + i // 2
            skip = (slab >= 2) & (info[4] == 0) & (rows_handed == 0)
            return (jnp.where(skip, info[1] * 2 + 1, info[slab] * 2 + lax.rem(i, 2)), 0)

        (acc,) = call(
            functools.partial(near_kernel, sizes, first, rows_handed, counts_in),
            "near",
            (info, *slabs, key_weight, value_weight),
            [HBM] * len(slabs) + [pl.BlockSpec((width // 2, cols), weights)] * 2,
            [f32((total, 2 * cols))],
            [pl.BlockSpec((total, 2 * cols), lambda i, info: (0, 0))],
            [pltpu.VMEM((last - first, total, width), jnp.bfloat16), dma((last - first, len(sizes)))],
            grid=(2 * (last - first),),
        )
        for i, c in enumerate(taken):
            accs.setdefault(c, []).append((acc, sum(sizes[:i])))

    def reach(*taken):
        sizes = [2 * CHUNKS[c][2] for c in taken]
        total = sum(sizes)
        (out,) = call(
            functools.partial(far_kernel, sizes),
            "far",
            (info, *(mr[c] for c in taken), *reached),
            [SMEM] + [HBM] * (len(taken) + len(reached)),
            [bf16((total, 2 * cols))],
            [VMEM],
            [
                pltpu.VMEM((8, total, 2 * share), jnp.bfloat16),
                pltpu.VMEM((8, *reached[0].shape), jnp.bfloat16),
                dma((8, 2, len(sizes))),
                dma((8,)),
            ],
        )
        out = move("far%d" % taken[0], out, outward)
        for i, c in enumerate(taken):
            far.setdefault(c, []).append((out, (sum(sizes[:i]), 0, 2 * cols)))

    def finish(*taken):
        segments, arrays, here = [], [], 0
        for c in taken:
            k, low, rows = CHUNKS[c]
            arrays += [a for a, _ in accs[c]] + [a for a, _ in far.get(c, [])]
            segments.append(
                Segment(low, rows, 2 * k, [r for _, r in accs[c]], here, 2 * c, [p for _, p in far.get(c, [])])
            )
            here += 2 * rows
        most_accs = max(len(s.accs) for s in segments)
        args = [plan, *arrays, *total_squares, key_bias[None, :], value_bias[None, :], cosine, sine, *done]
        done[:] = call(
            functools.partial(finish_kernel, segments, whole, bool(done)),
            "finish",
            tuple(args),
            [SMEM] + [HBM] * len(arrays) + [VMEM] * 4 + [HBM] * (2 + len(done)),
            [bf16((tokens, cols))] * 2,
            [HBM] * 2,
            [
                pltpu.VMEM((most_accs, here, 2 * cols), jnp.float32),
                pltpu.VMEM((here, 2 * cols), jnp.bfloat16),
                pltpu.VMEM((here, cols), jnp.bfloat16),
                pltpu.VMEM((here, cols), jnp.bfloat16),
                pltpu.VMEM((here, HD), jnp.float32),
                pltpu.VMEM((here, HD), jnp.float32),
                dma((len(segments), 4)),
                dma((len(segments), 2, 2)),
                dma((len(segments), 2, 2)),
            ],
            aliases={len(args) - 2: 0, len(args) - 1: 1} if done else None,
        )

    def both_ways(i):
        return [[(0, m, STEPS[i])] for m in (2, 3)]

    def exchange(i, sent):
        came[i] = {m: (move("a%d" % i, array, swap[m]), 0) for m, array in zip((2, 3), sent)}

    tables = [move("table", dest_table, swap[m]) for m in range(1, stores)]
    *s0, close = send(*both_ways(0), [(0, 1, (0, 0, BLOCK))])
    exchange(0, s0)
    beside = [move("b0", close, swap[1])]
    (plan,) = call(
        functools.partial(plan_kernel, stores, per_row),
        "plan",
        (dest_table, *tables),
        [SMEM] * stores,
        [jax.ShapeDtypeStruct((per_row, 4), jnp.int32)],
        [SMEM],
    )
    def join(axis, here, hopped, *before):
        return call(
            functools.partial(join_kernel, axis),
            "join",
            (info, here, hopped, *before),
            [SMEM] + [HBM] * (2 + axis),
            [bf16((2 * share, cols)), bf16((4 * share, cols))][: 1 + axis],
            [VMEM] * (1 + axis),
            [dma((3, 2))],
        )

    onward = [((k - 1) * BLOCK, 3, (k, 0, BLOCK)) for k in range(1, most)]
    onward += [((most + k - 2) * BLOCK, 1, (k, 0, BLOCK)) for k in range(1, most)]
    *s1, passed = send(*both_ways(1), onward)
    exchange(1, s1)
    passed = move("pass", passed, swap[1])
    beside.append(passed)
    prep(0, FAR)
    pass_own(0)
    packs = call(
        functools.partial(pack_kernel, per_row),
        "pack",
        (dest_table, cached, passed),
        [SMEM, HBM, HBM],
        [bf16((2 * BLOCK, width))] * 3,
        [VMEM] * 3,
        [dma((3, 2))],
    )

    def hop(k, pack):
        hopped = move("h%d" % k, pack, swap[2])
        came[k + 1] = {2: (hopped, 0), 3: (hopped, BLOCK)}

    prep(1)
    pass_own(1)
    hop(1, packs[0])
    cuts = call(
        cut_kernel, "cut", (key_weight, value_weight), [HBM] * 2, [bf16((share, cols))] * 2, [VMEM] * 2, [dma((2,))]
    )

    lent_k = move("ink", cuts[0], inward)
    relay(0)
    relay(1)
    prep(2)
    pass_own(2)
    (pack,) = pin(packs[1])
    hop(2, pack)
    (positions,) = call(
        copy_kernel, "copy", (positions,), [VMEM], [jax.ShapeDtypeStruct(positions.shape, jnp.int32)], [VMEM]
    )
    cosine, sine = pin(*rope_tables(positions))
    mr[0], lent_k, lent_v = pin(mr[0], lent_k, cuts[1])
    hand(0)
    lent_v = move("inv", lent_v, inward)
    near((0, 1), 0, 2)
    relay(2)
    prep(3)
    pass_own(3)
    mr[1], pack = pin(mr[1], packs[2])
    hop(3, pack)
    fw[0], lent_v, lent_k, mr[1] = pin(fw[0], lent_v, lent_k, mr[1])
    hand(1)
    came_k = move("wk1", lent_k, across)
    (lent_v,) = pin(lent_v)
    came_v = move("wv1", lent_v, swap[2])
    near((2,), 0, 2)
    relay(3)
    (mr[2],) = pin(mr[2])
    prep(4)
    squares = sums(0, *(ssq[c] for c in range(len(CHUNKS))))
    paired = move("half", squares, pair)
    fw[1], own[4] = pin(fw[1], own[4])
    pass_own(4)
    (joined_k,) = join(0, lent_k, came_k)
    came_k = move("wk2", joined_k, swap[2])
    joined_v, joined = join(1, lent_v, came_v, joined_k)
    came_v = move("wv2", joined_v, across)
    mr[2], paired = pin(mr[2], paired)
    hand(2)
    near((3, 4), 0, 2)
    (mr[3],) = pin(mr[3])
    squares = sums(1, squares, paired)
    rest = move("rest", squares, ends)
    relay(4)
    near((0, 1), 2, 4)
    came_k, came_v, joined = pin(came_k, came_v, joined)
    beside_w = [move("core", w, swap[1]) for w in (joined, came_k, came_v)]
    total_squares = (squares, rest)
    finish(0, 1)
    (fw[2],) = pin(fw[2], cost=FAR)
    reached = (joined_k, joined_v, came_k, came_v, *beside_w)
    reach(3)
    reach(4)
    near((2, 3, 4), 2, 4)
    finish(2, 3)
    finish(4)
    return tuple(done)


def slot_ranks(dest_table, counts, per_row):
    slot_ids = jnp.arange(dest_table.shape[1], dtype=jnp.int32)
    is_valid = slot_ids[None, :] < counts[:, None]
    row_ids = jnp.where(is_valid, dest_table // per_row, -1)
    earlier = (
        (row_ids[:, :, None] == row_ids[:, None, :])
        & (slot_ids[None, None, :] < slot_ids[None, :, None])
        & is_valid[:, None, :]
    )
    return is_valid, row_ids, jnp.sum(earlier.astype(jnp.int32), axis=2)


def rotate_keys(key_raw, positions):
    rows, cols = key_raw.shape
    cosine, sine = rope_tables(positions)
    heads = key_raw.reshape(rows, cols // HD, HD)
    turned = heads * cosine[:, None, :] + jnp.roll(heads, HD // 2, axis=2) * sine[:, None, :]
    return turned.reshape(rows, cols)


def gathered(cached_rows, counts, dest_table, positions, norm_gain, key_weight, value_weight, key_bias, value_bias):
    stores = lax.axis_size("store")
    own_row = lax.axis_index("store")
    capacity = dest_table.shape[1]
    per_pair = capacity // stores
    per_row = positions.shape[0] // BLOCK
    width = cached_rows.shape[2]
    flat_slots = cached_rows.reshape(capacity, BLOCK * width)
    all_counts = lax.all_gather(counts, "store", axis=0, tiled=True)
    all_table = lax.all_gather(dest_table, "store", axis=0, tiled=True)
    is_valid, _, row_rank = slot_ranks(all_table, all_counts, per_row)
    target = own_row * per_row + jnp.arange(per_row, dtype=jnp.int32)
    own_valid, own_rows, own_rank = slot_ranks(dest_table, counts, per_row)
    pick = (
        own_valid[0][None, None, :]
        & (own_rows[0][None, None, :] == jnp.arange(stores, dtype=jnp.int32)[:, None, None])
        & (own_rank[0][None, None, :] == jnp.arange(per_pair, dtype=jnp.int32)[None, :, None])
    ).astype(jnp.bfloat16)
    outgoing = jnp.einsum("rkj,jf->rkf", pick, flat_slots, preferred_element_type=jnp.float32)
    arrived = lax.all_to_all(outgoing.astype(jnp.bfloat16), "store", split_axis=0, concat_axis=0, tiled=True)
    placing = (
        is_valid[None, :, :, None]
        & (all_table[None, :, :, None] == target[:, None, None, None])
        & (row_rank[None, :, :, None] == jnp.arange(per_pair, dtype=jnp.int32)[None, None, None, :])
    )
    placing = jnp.sum(placing.astype(jnp.int32), axis=2).astype(jnp.bfloat16)
    local = jnp.einsum("bsk,skf->bf", placing, arrived, preferred_element_type=jnp.float32)
    local = local.astype(jnp.bfloat16).reshape(per_row * BLOCK, width)
    rows = lax.all_gather(local, "tensor", axis=1, tiled=True).astype(jnp.float32)
    scale = lax.rsqrt(jnp.mean(rows * rows, axis=1) + EPS)
    normed = (rows * scale[:, None] * norm_gain[None, :]).astype(jnp.bfloat16)
    keys = jnp.dot(normed, key_weight, preferred_element_type=jnp.float32) + key_bias[None, :]
    values = jnp.dot(normed, value_weight, preferred_element_type=jnp.float32) + value_bias[None, :]
    return rotate_keys(keys, positions).astype(jnp.bfloat16), values.astype(jnp.bfloat16)


def solution(mesh):
    in_specs = (
        P(("groups", "store"), None, "tensor"),
        P(("groups", "store")),
        P(("groups", "store"), None),
        P(("groups", "store")),
        P(),
        P(None, "tensor"),
        P(None, "tensor"),
        P("tensor"),
        P("tensor"),
    )
    out_specs = (P(("groups", "store"), "tensor"), P(("groups", "store"), "tensor"))
    small = tuple(mesh.shape[axis] for axis in ("groups", "store", "tensor")) == (2, 4, 4)
    body = grouped if small else gathered
    return jax.shard_map(body, mesh=mesh, in_specs=in_specs, out_specs=out_specs, check_vma=False)
```

```python
import collections
import functools

import jax
import jax.numpy as jnp
from jax import lax
from jax.experimental import pallas as pl
from jax.experimental.pallas import tpu as pltpu
from jax.sharding import PartitionSpec as P

HD = 128
BLOCK = 128
ROPE_BASE = 1000000.0
EPS = 1e-06
MIB = 1 << 20
VMEM_LIMIT = 63 * MIB
COST = 35 * 10**8
FAR = 10**11
HBM = pl.BlockSpec(memory_space=pltpu.HBM)
SMEM = pl.BlockSpec(memory_space=pltpu.SMEM)
VMEM = pl.BlockSpec(memory_space=pltpu.VMEM)
TOKEN = jax.ShapeDtypeStruct((8, 128), jnp.int32)

STEPS = ((0, 0, 64), (0, 64, 64), (1, 0, 128), (2, 0, 128), (3, 0, 128))
CHUNKS = ((0, 0, 64), (0, 64, 64), (1, 0, 128), (2, 0, 128), (3, 0, 128))


def rope_tables(positions):
    half = HD // 2
    inverse = 1.0 / ROPE_BASE ** (jnp.arange(half, dtype=jnp.float32) * 2.0 / HD)
    angles = positions.astype(jnp.float32)[:, None] * inverse[None, :]
    cosine, sine = jnp.cos(angles), jnp.sin(angles)
    return (
        jnp.concatenate([cosine, cosine], axis=1),
        jnp.concatenate([-sine, sine], axis=1),
    )


class Chain:
    def __init__(self):
        self.token = None

    def __call__(self, kernel, name, args, specs, outs, out_specs, scratch=(), grid=None, aliases=None, cost=COST):
        first = self.token is None
        prefetch = 0 if grid is None else 1
        taken, given = len(args), len(outs)

        def body(*refs):
            ins = refs[:taken]
            after = taken + (0 if first else 1)
            kernel(*ins, *refs[after : after + given], *refs[after + given + 1 :])

        tokens = () if first else (self.token,)
        in_specs = list(specs) + [HBM] * len(tokens)
        out_specs = list(out_specs) + [HBM]
        if grid is None:
            where = dict(in_specs=in_specs, out_specs=out_specs, scratch_shapes=list(scratch))
        else:
            where = dict(
                grid_spec=pltpu.PrefetchScalarGridSpec(
                    num_scalar_prefetch=prefetch,
                    grid=grid,
                    in_specs=in_specs,
                    out_specs=out_specs,
                    scratch_shapes=list(scratch),
                )
            )
        result = pl.pallas_call(
            body,
            out_shape=tuple(outs) + (TOKEN,),
            input_output_aliases=aliases or {},
            compiler_params=pltpu.CompilerParams(vmem_limit_bytes=VMEM_LIMIT),
            cost_estimate=pl.CostEstimate(flops=cost, bytes_accessed=1, transcendentals=0),
            name=name,
            **where,
        )(*args, *tokens)
        self.token = result[-1]
        return result[:-1]

    def pin(self, name, arrays, cost=COST):
        outs = [jax.ShapeDtypeStruct(a.shape, a.dtype) for a in arrays]
        n = len(arrays)
        return self(
            lambda *refs: None, name, arrays, [HBM] * n, outs, [HBM] * n, aliases={i: i for i in range(n)}, cost=cost
        )


def in_row(table, low, per_row):
    start, count = jnp.int32(0), jnp.int32(0)
    for s in range(table.shape[1]):
        block = table[0, s]
        start += ((block >= 0) & (block < low)).astype(jnp.int32)
        count += ((block >= low) & (block < low + per_row)).astype(jnp.int32)
    return start, count


def plan_kernel(stores, per_row, *refs):
    tables, plan = refs[:-1], refs[-1]
    low = lax.axis_index("store") * per_row
    spans = [in_row(t, low, per_row) for t in tables]
    n = jnp.int32(0)
    for i in range(per_row):
        for f in range(3):
            plan[i, f] = jnp.int32(0)
    for r in range(tables[0].shape[1] // stores):
        for m in range(stores):
            start, count = spans[m]
            valid = r < count

            @pl.when(valid)
            def _():
                plan[n, 0] = jnp.int32(r * stores + m)
                plan[n, 1] = start + r
                plan[n, 2] = tables[m][0, start + r] - low

            n += valid.astype(jnp.int32)


def send_kernel(steps, per_row, table, cached, *refs):
    outs, sems = refs[:-1], refs[-1]
    own_row = lax.axis_index("store")
    last = table.shape[1] - 1
    starts = {m: in_row(table, (own_row ^ m) * per_row, per_row)[0] for m in {m for s in steps for _, m, _ in s}}
    copies = []
    for out, parts in zip(outs, steps):
        for at, m, (k, low, rows) in parts:
            src = pl.multiple_of(jnp.minimum(starts[m] + k, last) * BLOCK + low, 16)
            copies.append(
                pltpu.make_async_copy(cached.at[pl.ds(src, rows)], out.at[pl.ds(at, rows)], sems.at[len(copies)])
            )
            copies[-1].start()
    for c in copies:
        c.wait()


def pack_kernel(per_row, table, cached, passed, *refs):
    outs, sems = refs[:-1], refs[-1]
    start, _ = in_row(table, (lax.axis_index("store") ^ 2) * per_row, per_row)
    copies = []
    for i, out in enumerate(outs):
        src = pl.multiple_of(jnp.minimum(start + i + 1, table.shape[1] - 1) * BLOCK, 16)
        copies.append(pltpu.make_async_copy(cached.at[pl.ds(src, BLOCK)], out.at[pl.ds(0, BLOCK)], sems.at[i, 0]))
        here = passed.at[pl.ds(i * BLOCK, BLOCK)]
        copies.append(pltpu.make_async_copy(here, out.at[pl.ds(BLOCK, BLOCK)], sems.at[i, 1]))
    for c in copies:
        c.start()
    for c in copies:
        c.wait()


def cut_kernel(key_weight, value_weight, *refs):
    outs, sems = refs[:-1], refs[-1]
    z, y, own_row = lax.axis_index("tensor"), lax.axis_index("groups"), lax.axis_index("store")
    share = outs[0].shape[0]
    slab = jnp.where(z == 0, 2 + y, 1 - y)
    at = pl.multiple_of((slab * 4 + own_row) * share, 128)
    copies = [
        pltpu.make_async_copy(weight.at[pl.ds(at, share)], out, sems.at[g])
        for g, (weight, out) in enumerate(zip((key_weight, value_weight), outs))
    ]
    for c in copies:
        c.start()
    for c in copies:
        c.wait()


def join_kernel(axis, info, here, came, *refs):
    before, outs, sems = refs[:axis], refs[axis:-1], refs[-1]
    share = here.shape[0]
    place = info[5 + axis]
    copies = []
    for t, src in enumerate((here, came)):
        at = pl.multiple_of((place if t == 0 else 1 - place) * share, 128)
        copies.append(pltpu.make_async_copy(src, outs[0].at[pl.ds(at, share)], sems.at[0, t]))
        if axis == 1:
            copies.append(pltpu.make_async_copy(src, outs[1].at[pl.ds(at + 2 * share, share)], sems.at[1, t]))
    if axis == 1:
        copies.append(pltpu.make_async_copy(before[0], outs[1].at[pl.ds(0, 2 * share)], sems.at[2, 0]))
    for c in copies:
        c.start()
    for c in copies:
        c.wait()


def prep_kernel(low, rows, first, stores, pieces, plan, cached, *refs):
    arrived = refs[: len(pieces)]
    gain, y_out, ssq_out, held, sems = refs[len(pieces) :]
    width = held.shape[2]
    z = lax.axis_index("tensor")
    for j in range(2):
        code = plan[first + j, 0]

        @pl.when(lax.rem(code, stores) == 0)
        def _():
            start = pl.multiple_of(plan[first + j, 1] * BLOCK + low, 16)
            pltpu.make_async_copy(cached.at[pl.ds(start, rows)], held.at[j], sems.at[j]).start()

        for (r, m, p_low, p_rows, at), ref in zip(pieces, arrived):
            a, b = max(low, p_low), min(low + rows, p_low + p_rows)

            @pl.when(code == r * stores + m)
            def _():
                pltpu.make_async_copy(
                    ref.at[pl.ds(at + a - p_low, b - a)], held.at[j, pl.ds(a - low, b - a)], sems.at[j]
                ).start()

    for j in range(2):
        pltpu.make_async_copy(cached.at[pl.ds(0, rows)], held.at[j], sems.at[j]).wait()
        sums = jnp.zeros((rows, 128), jnp.float32)
        for c in range(0, width, 128):
            x = held[j, :, c : c + 128].astype(jnp.float32)
            here = gain[:, pl.ds(pl.multiple_of(z * width + c, 128), 128)]
            y_out[j * rows : (j + 1) * rows, c : c + 128] = (x * here).astype(jnp.bfloat16)
            sums += x * x
        ssq_out[j : j + 1, :rows] = jnp.sum(sums.T, axis=0, keepdims=True)


def copy_kernel(given, out):
    out[...] = given[...]


def sums_kernel(step, *refs):
    out = refs[-1]
    if step == 0:
        out[...] = jnp.zeros_like(out)
        for i, ref in enumerate(refs[:-1]):
            out[2 * i : 2 * i + 2, :] = ref[...]
    else:
        out[...] = refs[0][...] + refs[1][...]


def relay_kernel(own, ex, out, sems):
    rows = own.shape[0]
    copies = [
        pltpu.make_async_copy(src, out.at[pl.ds(i * rows, rows)], sems.at[i]) for i, src in enumerate((own, ex))
    ]
    for c in copies:
        c.start()
    for c in copies:
        c.wait()


def near_kernel(sizes, first, lead, counts, info, *refs):
    n = len(sizes)
    wk, wv, acc, acts, sems = refs[-5:]
    arrays = [refs[sum(counts[:c]) : sum(counts[: c + 1])] for c in range(n)]
    slabs = acts.shape[0]
    i = pl.program_id(0)
    slab, half = first + i // 2, lax.rem(i, 2)
    inner = info[4] == 1
    starts = [sum(sizes[:c]) for c in range(n)]

    def copies(s, which, skip=0, rows=sum(sizes)):
        return [
            pltpu.make_async_copy(
                arrays[c][which].at[pl.ds(skip * sizes[c], sizes[c])],
                acts.at[s - first, pl.ds(starts[c], sizes[c])],
                sems.at[s - first, c],
            )
            for c in range(n)
            if starts[c] < rows
        ]

    def held(s, fetch):
        if s < 2:
            fetch(copies(s, s))
        else:

            @pl.when(inner)
            def _():
                fetch(copies(s, 2 - first, s - 2))

            if lead:

                @pl.when(jnp.logical_not(inner))
                def _():
                    fetch(copies(s, 3 - first, s - 2, lead))

    def start(made):
        for c in made:
            c.start()

    def wait(made):
        for c in made:
            c.wait()

    @pl.when(i == 0)
    def _():
        for s in range(first, first + slabs):
            held(s, start)

    for s in range(first, first + slabs):

        @pl.when((half == 0) & (slab == s))
        def _():
            held(s, wait)

    part, cols = wk.shape

    @pl.when(i == 0)
    def _():
        acc[...] = jnp.zeros_like(acc)

    def add(rows):
        a = acts[slab - first, :rows, pl.ds(pl.multiple_of(half * part, part), part)]
        acc[:rows, :cols] += jnp.dot(a, wk[...], preferred_element_type=jnp.float32)
        acc[:rows, cols:] += jnp.dot(a, wv[...], preferred_element_type=jnp.float32)

    whole_rows = (slab < 2) | inner if lead < sum(sizes) else i >= 0

    @pl.when(whole_rows)
    def _():
        add(sum(sizes))

    if 0 < lead < sum(sizes):

        @pl.when(jnp.logical_not(whole_rows))
        def _():
            add(lead)


def far_kernel(sizes, info, *refs):
    n = len(sizes)
    slabs = refs[:n]
    joined_k, joined_v, came_k, came_v, joined, beside_k, beside_v = refs[n : n + 7]
    out, acts, held, act_sems, sems = refs[n + 7 :]
    starts = [sum(sizes[:c]) for c in range(n)]
    rows, cols = held.shape[1:]
    share = rows // 2
    weights = (joined_k, came_k, joined.at[pl.ds(0, rows)], beside_k)
    weights += (joined_v, came_v, joined.at[pl.ds(rows, rows)], beside_v)
    y, x, core = info[5], info[6], info[7]

    @pl.when(info[4] == 1)
    def _():
        loads = []
        for g in range(2):
            for i in range(4):
                here = core if i < 2 else 1 - core
                for t in range(2):
                    if g == 0:
                        slab, chip = t, (x if i % 2 == 0 else 1 - x)
                    else:
                        slab, chip = (y if i % 2 == 0 else 1 - y), t
                    at = pl.multiple_of((2 * chip + here) * share, 128)
                    for c in range(n):
                        row = pl.multiple_of(slab * sizes[c], 16)
                        loads.append(
                            pltpu.make_async_copy(
                                slabs[c].at[pl.ds(row, sizes[c]), pl.ds(at, share)],
                                acts.at[4 * g + i, pl.ds(starts[c], sizes[c]), pl.ds(t * share, share)],
                                act_sems.at[4 * g + i, t, c],
                            )
                        )
        copies = [pltpu.make_async_copy(w, held.at[i], sems.at[i]) for i, w in enumerate(weights)]
        for i, c in enumerate(copies):
            for load in loads[2 * n * i : 2 * n * (i + 1)]:
                load.start()
            c.start()
        for g in range(2):
            total = None
            for i in range(4 * g, 4 * g + 4):
                for load in loads[2 * n * i : 2 * n * (i + 1)]:
                    load.wait()
                copies[i].wait()
                term = jnp.dot(acts[i], held[i], preferred_element_type=jnp.float32)
                total = term if total is None else total + term
            out[:, g * cols : (g + 1) * cols] = total.astype(jnp.bfloat16)


def finish_kernel(segments, whole, chained, plan, *refs):
    given = []
    at = 0
    for s in segments:
        n = len(s.accs) + len(s.parts)
        given.append(refs[at : at + n])
        at += n
    ssq_a, ssq_b, bk, bv, cosine, sine = refs[at : at + 6]
    refs = refs[at + 6 + (2 if chained else 0) :]
    k_out, v_out, acc_held, far_held, k_held, v_held, cos_held, sin_held, in_sems, rope_sems, out_sems = refs
    cols = k_held.shape[1]
    loads, spots = [], []
    for i, (s, arrays) in enumerate(zip(segments, given)):
        rows, here, count = s.rows, s.here, 2 * s.rows
        mine = [
            pltpu.make_async_copy(ref.at[pl.ds(row, count)], acc_held.at[t, pl.ds(here, count)], in_sems.at[i, t])
            for t, (row, ref) in enumerate(zip(s.accs, arrays))
        ]
        for p, ((row, col, wide), ref) in enumerate(zip(s.parts, arrays[len(s.accs) :])):
            mine.append(
                pltpu.make_async_copy(
                    ref.at[pl.ds(row, count)],
                    far_held.at[pl.ds(here, count), pl.ds(col, wide)],
                    in_sems.at[i, 2 + p],
                )
            )
        spots.append([pl.multiple_of(plan[s.first + j, 2] * BLOCK + s.low, 16) for j in range(2)])
        for j in range(2):
            for t, (src, dst) in enumerate(((cosine, cos_held), (sine, sin_held))):
                mine.append(
                    pltpu.make_async_copy(
                        src.at[pl.ds(spots[i][j], rows)], dst.at[pl.ds(here + j * rows, rows)], rope_sems.at[i, j, t]
                    )
                )
        for c in mine:
            c.start()
        loads.append(mine)
    stores = []
    for i, s in enumerate(segments):
        rows = s.rows
        for c in loads[i]:
            c.wait()
        for j in range(2):
            row = s.ssq + j
            sums = jnp.broadcast_to(ssq_a[row : row + 1, :] + ssq_b[row : row + 1, :], (8, BLOCK))
            scale = lax.rsqrt(sums.T[:rows, :1] * (1.0 / whole) + EPS)
            span = slice(s.here + j * rows, s.here + (j + 1) * rows)
            cos_rows, sin_rows = cos_held[span, :], sin_held[span, :]
            for h in range(cols // HD):
                lanes = slice(h * HD, (h + 1) * HD)
                k = acc_held[0, span, lanes]
                if len(s.accs) > 1:
                    k += acc_held[1, span, lanes]
                if s.parts:
                    k += far_held[span, lanes].astype(jnp.float32)
                k = k * scale + bk[:, lanes]
                k_held[span, lanes] = (k * cos_rows + pltpu.roll(k, HD // 2, 1) * sin_rows).astype(jnp.bfloat16)
                lanes_v = slice(cols + h * HD, cols + (h + 1) * HD)
                v = acc_held[0, span, lanes_v]
                if len(s.accs) > 1:
                    v += acc_held[1, span, lanes_v]
                if s.parts:
                    v += far_held[span, lanes_v].astype(jnp.float32)
                v_held[span, lanes] = (v * scale + bv[:, lanes]).astype(jnp.bfloat16)
            for t, (held, out) in enumerate(((k_held, k_out), (v_held, v_out))):
                stores.append(
                    pltpu.make_async_copy(
                        held.at[pl.ds(s.here + j * rows, rows)],
                        out.at[pl.ds(spots[i][j], rows)],
                        out_sems.at[i, j, t],
                    )
                )
                stores[-1].start()
    for c in stores:
        c.wait()


Segment = collections.namedtuple(
    "Segment", ("low", "rows", "first", "accs", "here", "ssq", "parts")
)


def grouped(cached_rows, counts, dest_table, positions, norm_gain, key_weight, value_weight, key_bias, value_bias):
    stores = lax.axis_size("store")
    z, y = lax.axis_index("tensor"), lax.axis_index("groups")
    tokens = positions.shape[0]
    per_row = tokens // BLOCK
    most = dest_table.shape[1] // stores
    cached = cached_rows[0]
    width = cached.shape[1]
    whole, cols = key_weight.shape
    share = whole // 16
    dma = pltpu.SemaphoreType.DMA
    bf16 = functools.partial(jax.ShapeDtypeStruct, dtype=jnp.bfloat16)
    f32 = functools.partial(jax.ShapeDtypeStruct, dtype=jnp.float32)
    swap = {m: ("store", [(s, s ^ m) for s in range(stores)]) for m in range(1, stores)}
    pair = ("tensor", [(0, 1), (1, 0), (2, 3), (3, 2)])
    middle = ("tensor", [(1, 2), (2, 1)])
    inward = ("tensor", [(0, 1), (3, 2)])
    outward = ("tensor", [(1, 0), (2, 3)])
    across = ("groups", [(0, 1), (1, 0)])
    ends = ("tensor", [(0, 3), (1, 2), (2, 1), (3, 0)])

    inner = (z == 1) | (z == 2)
    other = [jnp.where(inner, 3 - z, z ^ 2), jnp.where(inner, (3 - z) ^ 1, 3 - z)]
    chip, core = lax.axis_index("store") // 2, lax.rem(lax.axis_index("store"), 2)
    info = jnp.stack([z, z ^ 1, *other, inner.astype(jnp.int32), y, chip, core]).astype(jnp.int32)
    gain = norm_gain[None, :]

    call = Chain()
    came, own, ssq, ex, mr, fw, accs, far = {}, {}, {}, {}, {}, {}, {}, {}
    done = []

    def move(label, array, way):
        with jax.named_scope(label):
            return lax.ppermute(array, *way)

    def send(*parts):
        shapes = [bf16((sum(s[2] for _, _, s in p), width)) for p in parts]
        return call(
            functools.partial(send_kernel, parts, per_row),
            "send",
            (dest_table, cached),
            [SMEM, HBM],
            shapes,
            [VMEM] * len(shapes),
            [dma((sum(len(p) for p in parts),))],
        )

    def prep(c, cost=COST):
        k, low, rows = CHUNKS[c]
        pieces, arrays = [], []
        for r in range(k + 1):
            pieces.append((r, 1, 0, BLOCK, 0 if r == 0 else (most + r - 2) * BLOCK))
            arrays.append(beside[min(r, 1)])
        for i, (r, p_low, p_rows) in enumerate(STEPS):
            if r <= k and p_low < low + rows and low < p_low + p_rows:
                for m in (2, 3):
                    array, at = came[i][m]
                    pieces.append((r, m, p_low, p_rows, at))
                    arrays.append(array)
        own[c], ssq[c] = call(
            functools.partial(prep_kernel, low, rows, 2 * k, stores, pieces),
            "prep",
            (plan, cached, *arrays, gain),
            [SMEM, HBM] + [HBM] * len(pieces) + [VMEM],
            [bf16((2 * rows, width)), f32((2, BLOCK))],
            [VMEM, VMEM],
            [pltpu.VMEM((2, rows, width), jnp.bfloat16), dma((2,))],
            cost=cost,
        )

    def pass_own(c):
        ex[c] = move("ex%d" % c, own[c], pair)

    def relay(c):
        rows = 2 * CHUNKS[c][2]
        (both,) = call(
            relay_kernel, "relay", (own[c], ex[c]), [HBM] * 2, [bf16((2 * rows, width))], [VMEM], [dma((2,))]
        )
        mr[c] = move("mr%d" % c, both, middle)

    def pin(*arrays, cost=COST):
        return call.pin("pin", arrays, cost)

    def hand(c):
        fw[c] = move("fw%d" % c, mr[c], outward)

    def sums(step, *arrays):
        (out,) = call(
            functools.partial(sums_kernel, step), "sums", arrays, [VMEM] * len(arrays), [f32((16, BLOCK))], [VMEM]
        )
        return out

    handed = (0, 1, 2)

    def near(taken, first, last):
        sizes = [2 * CHUNKS[c][2] for c in taken]
        total = sum(sizes)
        rows_handed = sum(size for c, size in zip(taken, sizes) if last == 4 and c in handed)
        kinds = ((own, ex) if first == 0 else ()) + ((mr,) if last == 4 else ())
        groups = [[k[c] for k in kinds] + ([fw[c]] if last == 4 and c in handed else []) for c in taken]
        slabs = [array for group in groups for array in group]
        counts_in = [len(group) for group in groups]

        def weights(i, info):
            slab = first + i // 2
            skip = (slab >= 2) & (info[4] == 0) & (rows_handed == 0)
            return (jnp.where(skip, info[1] * 2 + 1, info[slab] * 2 + lax.rem(i, 2)), 0)

        (acc,) = call(
            functools.partial(near_kernel, sizes, first, rows_handed, counts_in),
            "near",
            (info, *slabs, key_weight, value_weight),
            [HBM] * len(slabs) + [pl.BlockSpec((width // 2, cols), weights)] * 2,
            [f32((total, 2 * cols))],
            [pl.BlockSpec((total, 2 * cols), lambda i, info: (0, 0))],
            [pltpu.VMEM((last - first, total, width), jnp.bfloat16), dma((last - first, len(sizes)))],
            grid=(2 * (last - first),),
        )
        for i, c in enumerate(taken):
            accs.setdefault(c, []).append((acc, sum(sizes[:i])))

    def reach(*taken):
        sizes = [2 * CHUNKS[c][2] for c in taken]
        total = sum(sizes)
        (out,) = call(
            functools.partial(far_kernel, sizes),
            "far",
            (info, *(mr[c] for c in taken), *reached),
            [SMEM] + [HBM] * (len(taken) + len(reached)),
            [bf16((total, 2 * cols))],
            [VMEM],
            [
                pltpu.VMEM((8, total, 2 * share), jnp.bfloat16),
                pltpu.VMEM((8, *reached[0].shape), jnp.bfloat16),
                dma((8, 2, len(sizes))),
                dma((8,)),
            ],
        )
        out = move("far%d" % taken[0], out, outward)
        for i, c in enumerate(taken):
            far.setdefault(c, []).append((out, (sum(sizes[:i]), 0, 2 * cols)))

    def finish(*taken):
        segments, arrays, here = [], [], 0
        for c in taken:
            k, low, rows = CHUNKS[c]
            arrays += [a for a, _ in accs[c]] + [a for a, _ in far.get(c, [])]
            segments.append(
                Segment(low, rows, 2 * k, [r for _, r in accs[c]], here, 2 * c, [p for _, p in far.get(c, [])])
            )
            here += 2 * rows
        most_accs = max(len(s.accs) for s in segments)
        args = [plan, *arrays, *total_squares, key_bias[None, :], value_bias[None, :], cosine, sine, *done]
        done[:] = call(
            functools.partial(finish_kernel, segments, whole, bool(done)),
            "finish",
            tuple(args),
            [SMEM] + [HBM] * len(arrays) + [VMEM] * 4 + [HBM] * (2 + len(done)),
            [bf16((tokens, cols))] * 2,
            [HBM] * 2,
            [
                pltpu.VMEM((most_accs, here, 2 * cols), jnp.float32),
                pltpu.VMEM((here, 2 * cols), jnp.bfloat16),
                pltpu.VMEM((here, cols), jnp.bfloat16),
                pltpu.VMEM((here, cols), jnp.bfloat16),
                pltpu.VMEM((here, HD), jnp.float32),
                pltpu.VMEM((here, HD), jnp.float32),
                dma((len(segments), 4)),
                dma((len(segments), 2, 2)),
                dma((len(segments), 2, 2)),
            ],
            aliases={len(args) - 2: 0, len(args) - 1: 1} if done else None,
        )

    def both_ways(i):
        return [[(0, m, STEPS[i])] for m in (2, 3)]

    def exchange(i, sent):
        came[i] = {m: (move("a%d" % i, array, swap[m]), 0) for m, array in zip((2, 3), sent)}

    tables = [move("table", dest_table, swap[m]) for m in range(1, stores)]
    *s0, close = send(*both_ways(0), [(0, 1, (0, 0, BLOCK))])
    exchange(0, s0)
    beside = [move("b0", close, swap[1])]
    (plan,) = call(
        functools.partial(plan_kernel, stores, per_row),
        "plan",
        (dest_table, *tables),
        [SMEM] * stores,
        [jax.ShapeDtypeStruct((per_row, 4), jnp.int32)],
        [SMEM],
    )
    def join(axis, here, hopped, *before):
        return call(
            functools.partial(join_kernel, axis),
            "join",
            (info, here, hopped, *before),
            [SMEM] + [HBM] * (2 + axis),
            [bf16((2 * share, cols)), bf16((4 * share, cols))][: 1 + axis],
            [VMEM] * (1 + axis),
            [dma((3, 2))],
        )

    onward = [((k - 1) * BLOCK, 3, (k, 0, BLOCK)) for k in range(1, most)]
    onward += [((most + k - 2) * BLOCK, 1, (k, 0, BLOCK)) for k in range(1, most)]
    *s1, passed = send(*both_ways(1), onward)
    exchange(1, s1)
    passed = move("pass", passed, swap[1])
    beside.append(passed)
    prep(0, FAR)
    pass_own(0)
    packs = call(
        functools.partial(pack_kernel, per_row),
        "pack",
        (dest_table, cached, passed),
        [SMEM, HBM, HBM],
        [bf16((2 * BLOCK, width))] * 3,
        [VMEM] * 3,
        [dma((3, 2))],
    )

    def hop(k, pack):
        hopped = move("h%d" % k, pack, swap[2])
        came[k + 1] = {2: (hopped, 0), 3: (hopped, BLOCK)}

    prep(1)
    pass_own(1)
    hop(1, packs[0])
    cuts = call(
        cut_kernel, "cut", (key_weight, value_weight), [HBM] * 2, [bf16((share, cols))] * 2, [VMEM] * 2, [dma((2,))]
    )

    lent_k = move("ink", cuts[0], inward)
    relay(0)
    relay(1)
    prep(2)
    pass_own(2)
    (pack,) = pin(packs[1])
    hop(2, pack)
    (positions,) = call(
        copy_kernel, "copy", (positions,), [VMEM], [jax.ShapeDtypeStruct(positions.shape, jnp.int32)], [VMEM]
    )
    cosine, sine = pin(*rope_tables(positions))
    mr[0], lent_k, lent_v = pin(mr[0], lent_k, cuts[1])
    hand(0)
    lent_v = move("inv", lent_v, inward)
    near((0, 1), 0, 2)
    relay(2)
    prep(3)
    pass_own(3)
    mr[1], pack = pin(mr[1], packs[2])
    hop(3, pack)
    fw[0], lent_v, lent_k, mr[1] = pin(fw[0], lent_v, lent_k, mr[1])
    hand(1)
    came_k = move("wk1", lent_k, across)
    (lent_v,) = pin(lent_v)
    came_v = move("wv1", lent_v, swap[2])
    near((2,), 0, 2)
    relay(3)
    (mr[2],) = pin(mr[2])
    prep(4)
    squares = sums(0, *(ssq[c] for c in range(len(CHUNKS))))
    paired = move("half", squares, pair)
    fw[1], own[4] = pin(fw[1], own[4])
    pass_own(4)
    (joined_k,) = join(0, lent_k, came_k)
    came_k = move("wk2", joined_k, swap[2])
    joined_v, joined = join(1, lent_v, came_v, joined_k)
    came_v = move("wv2", joined_v, across)
    mr[2], paired = pin(mr[2], paired)
    hand(2)
    near((3, 4), 0, 2)
    (mr[3],) = pin(mr[3])
    squares = sums(1, squares, paired)
    rest = move("rest", squares, ends)
    relay(4)
    near((0, 1), 2, 4)
    came_k, came_v, joined = pin(came_k, came_v, joined)
    beside_w = [move("core", w, swap[1]) for w in (joined, came_k, came_v)]
    total_squares = (squares, rest)
    near((3,), 2, 4)
    (fw[2],) = pin(fw[2], cost=FAR)
    reached = (joined_k, joined_v, came_k, came_v, *beside_w)
    reach(3)
    reach(4)
    near((2, 4), 2, 4)
    finish(0, 1, 2, 3)
    finish(4)
    return tuple(done)


def slot_ranks(dest_table, counts, per_row):
    slot_ids = jnp.arange(dest_table.shape[1], dtype=jnp.int32)
    is_valid = slot_ids[None, :] < counts[:, None]
    row_ids = jnp.where(is_valid, dest_table // per_row, -1)
    earlier = (
        (row_ids[:, :, None] == row_ids[:, None, :])
        & (slot_ids[None, None, :] < slot_ids[None, :, None])
        & is_valid[:, None, :]
    )
    return is_valid, row_ids, jnp.sum(earlier.astype(jnp.int32), axis=2)


def rotate_keys(key_raw, positions):
    rows, cols = key_raw.shape
    cosine, sine = rope_tables(positions)
    heads = key_raw.reshape(rows, cols // HD, HD)
    turned = heads * cosine[:, None, :] + jnp.roll(heads, HD // 2, axis=2) * sine[:, None, :]
    return turned.reshape(rows, cols)


def gathered(cached_rows, counts, dest_table, positions, norm_gain, key_weight, value_weight, key_bias, value_bias):
    stores = lax.axis_size("store")
    own_row = lax.axis_index("store")
    capacity = dest_table.shape[1]
    per_pair = capacity // stores
    per_row = positions.shape[0] // BLOCK
    width = cached_rows.shape[2]
    flat_slots = cached_rows.reshape(capacity, BLOCK * width)
    all_counts = lax.all_gather(counts, "store", axis=0, tiled=True)
    all_table = lax.all_gather(dest_table, "store", axis=0, tiled=True)
    is_valid, _, row_rank = slot_ranks(all_table, all_counts, per_row)
    target = own_row * per_row + jnp.arange(per_row, dtype=jnp.int32)
    own_valid, own_rows, own_rank = slot_ranks(dest_table, counts, per_row)
    pick = (
        own_valid[0][None, None, :]
        & (own_rows[0][None, None, :] == jnp.arange(stores, dtype=jnp.int32)[:, None, None])
        & (own_rank[0][None, None, :] == jnp.arange(per_pair, dtype=jnp.int32)[None, :, None])
    ).astype(jnp.bfloat16)
    outgoing = jnp.einsum("rkj,jf->rkf", pick, flat_slots, preferred_element_type=jnp.float32)
    arrived = lax.all_to_all(outgoing.astype(jnp.bfloat16), "store", split_axis=0, concat_axis=0, tiled=True)
    placing = (
        is_valid[None, :, :, None]
        & (all_table[None, :, :, None] == target[:, None, None, None])
        & (row_rank[None, :, :, None] == jnp.arange(per_pair, dtype=jnp.int32)[None, None, None, :])
    )
    placing = jnp.sum(placing.astype(jnp.int32), axis=2).astype(jnp.bfloat16)
    local = jnp.einsum("bsk,skf->bf", placing, arrived, preferred_element_type=jnp.float32)
    local = local.astype(jnp.bfloat16).reshape(per_row * BLOCK, width)
    rows = lax.all_gather(local, "tensor", axis=1, tiled=True).astype(jnp.float32)
    scale = lax.rsqrt(jnp.mean(rows * rows, axis=1) + EPS)
    normed = (rows * scale[:, None] * norm_gain[None, :]).astype(jnp.bfloat16)
    keys = jnp.dot(normed, key_weight, preferred_element_type=jnp.float32) + key_bias[None, :]
    values = jnp.dot(normed, value_weight, preferred_element_type=jnp.float32) + value_bias[None, :]
    return rotate_keys(keys, positions).astype(jnp.bfloat16), values.astype(jnp.bfloat16)


def solution(mesh):
    in_specs = (
        P(("groups", "store"), None, "tensor"),
        P(("groups", "store")),
        P(("groups", "store"), None),
        P(("groups", "store")),
        P(),
        P(None, "tensor"),
        P(None, "tensor"),
        P("tensor"),
        P("tensor"),
    )
    out_specs = (P(("groups", "store"), "tensor"), P(("groups", "store"), "tensor"))
    small = tuple(mesh.shape[axis] for axis in ("groups", "store", "tensor")) == (2, 4, 4)
    body = grouped if small else gathered
    return jax.shard_map(body, mesh=mesh, in_specs=in_specs, out_specs=out_specs, check_vma=False)
```
